768 devices in a mesh: ctx: 96 (over z, y), head: 8 (over x, core).
Axes of the slice: x: 4, y: 8, z: 12, core: 2. Of those that a mesh axis runs over, the one named last changes fastest.
Arguments:
- text_qkv: bfloat16 [12288, 3, 8192], P('ctx', None, 'head'), may hold values from -6 to 6
- vis_feats: bfloat16 [384, 1024], P('ctx'), may hold values from -6 to 6
- w_visual: bfloat16 [1024, 3, 8192], P(None, None, 'head'), may hold values from -0.1875 to 0.1875
- vis_src: int32 [12288], P('ctx'), may hold values from -1 to 383, as said below
- log_decay: float32 [64, 12288], P('head', 'ctx'), as said below
- norm_gain: float32 [8192], P('head'), may hold values from 0.5 to 1.5
Outputs:
- attn_out: bfloat16 [12288, 8192], P('ctx', 'head')
The draws below stay inside these ranges and needn't reach their ends.
Inputs may be any that keep to these rules, and one draw needn't show every extreme that they name: `vis_src`: -1 marks a text position; any other value is the row of vis_feats placed at that position; each of the 384 rows is placed at exactly one position; positions 0 and 1 are visual and take the rows 192 and 383; the later visual positions, in order along the sequence, take the rows 193 to 382 and then 0 to 191. `log_decay`: at most 0; differs from position to position.
All inputs are finite; a program needn't handle non-finite values.
Results may differ from the reference program's by a relative error of at most 0.0034.
Values may be sent and summed in bfloat16 or wider, within the bound.
A program may use at most 128 MiB of HBM per device.

```python
import jax
import jax.numpy as jnp
from jax import lax

HEAD_TOTAL = 64
HD = 128
VW = 1024
S_DEV = 128
SEQUENCE_TOKENS = 12288
VIS_ROWS = 384
INNER = 8192


def draw_vis_src(key, part):
    key = jax.random.fold_in(key, 11)
    key_base, key_scale = jax.random.split(key)
    shard_count = SEQUENCE_TOKENS // S_DEV
    baseline_sample = jax.random.randint(key_base, (SEQUENCE_TOKENS,), 0, 4096)
    length_factor = jax.random.randint(key_scale, (shard_count,), 1, 3)
    token_places = jnp.arange(SEQUENCE_TOKENS)
    partition_index = token_places // S_DEV
    extra_amount = jnp.where(token_places < 2, 16384, 0)
    ranking_value = (baseline_sample * length_factor[partition_index] + extra_amount) * SEQUENCE_TOKENS + token_places
    ordering = jnp.argsort(-ranking_value, stable=True)
    chosen = ordering[:VIS_ROWS]
    marked = jnp.zeros((SEQUENCE_TOKENS,), jnp.int32).at[chosen].set(1)
    ranks = jnp.cumsum(marked) - 1
    half_rows = VIS_ROWS // 2
    rotated = jnp.where(ranks == 0, half_rows, jnp.where(ranks == 1, VIS_ROWS - 1, jnp.where(ranks < half_rows, ranks - 1 + half_rows, ranks - half_rows)))
    return jnp.where(marked > 0, rotated, -1).astype(jnp.int32)


def draw_log_decay(key, part):
    key = jax.random.fold_in(key, 23)
    key_sequence = jax.random.split(key, 7)
    slow_low, slow_high = (0.05 / SEQUENCE_TOKENS, 0.5 / SEQUENCE_TOKENS)
    fast_low, fast_high = (1.0 / (2.0 * S_DEV), 1.0 / 30.0)
    shard_count = SEQUENCE_TOKENS // S_DEV
    slow_pick = jax.random.randint(key_sequence[0], (HEAD_TOTAL, 1), 0, 2) > 0
    slow_rate = jnp.exp(jax.random.uniform(key_sequence[1], (HEAD_TOTAL, 1), minval=jnp.log(slow_low), maxval=jnp.log(slow_high)))
    fast_rate = jnp.exp(jax.random.uniform(key_sequence[2], (HEAD_TOTAL, 1), minval=jnp.log(fast_low), maxval=jnp.log(fast_high)))
    head_decay_rate = jnp.where(slow_pick, slow_rate, fast_rate)
    device_split_factor = jnp.exp(jax.random.uniform(key_sequence[3], (HEAD_TOTAL, shard_count), minval=jnp.log(0.5), maxval=jnp.log(1.5)))
    device_split_factor = jnp.repeat(device_split_factor, S_DEV, axis=1)
    token_multiplier = jax.random.uniform(key_sequence[4], (HEAD_TOTAL, SEQUENCE_TOKENS), minval=0.5, maxval=1.5)
    token_groups = jax.random.randint(key_sequence[5], (HEAD_TOTAL, SEQUENCE_TOKENS), 0, SEQUENCE_TOKENS) < 3
    group_length = jax.random.uniform(key_sequence[6], (HEAD_TOTAL, SEQUENCE_TOKENS), minval=0.22, maxval=0.69)
    return (-(head_decay_rate * device_split_factor * token_multiplier) - jnp.where(token_groups, group_length, 0.0)).astype(jnp.float32)


def shard_levels(key, shape, cuts, low, high):
    def one(dim, shards_of):
        draws = jax.random.uniform(jax.random.fold_in(jax.random.fold_in(key, 6), dim), (shards_of,), jnp.float32, low / len(cuts), high / len(cuts))
        return jnp.repeat(jnp.exp(draws), shape[dim] // shards_of).reshape((-1,) + (1,) * (len(shape) - dim - 1))

    factor_of = one(*cuts[0])
    for cut in cuts[1:]:
        factor_of = factor_of * one(*cut)
    return factor_of


def noise(own_key, shape, width, bound, pieces=(), kind=jnp.bfloat16):
    array = jax.random.normal(own_key, shape, jnp.float32) * width
    if len(pieces) > 0:
        array = shard_levels(own_key, shape, pieces, -0.22, 0.18) * array
    return jnp.clip(array, min=-bound, max=bound).astype(kind)


def setup_inputs(seed: int = 0) -> dict:
    streams_of = jax.random.split(jax.random.key(seed), 7)
    return {
        "text_qkv": noise(streams_of[0], (SEQUENCE_TOKENS, 3, INNER), 1.0, 6.0, ((0, 96), (2, 8))),
        "vis_feats": noise(streams_of[1], (VIS_ROWS, VW), 1.0, 6.0, ((0, 96),)),
        "w_visual": noise(streams_of[2], (VW, 3, INNER), VW ** -0.5, 0.1875, ((2, 8),)),
        "vis_src": draw_vis_src(jax.random.fold_in(streams_of[6], 71), 0),
        "log_decay": draw_log_decay(jax.random.fold_in(streams_of[6], 71), 0),
        "norm_gain": jnp.clip(1.0 + 0.1 * jax.random.normal(streams_of[5], (INNER,), jnp.float32), 0.5, 1.5),
    }


def reference(text_qkv, vis_feats, w_visual, vis_src, log_decay, norm_gain):
    highest = lax.Precision.HIGHEST
    inner_width = HEAD_TOTAL * HD
    flat_weight = w_visual.reshape(VW, 3 * inner_width)
    visual_qkv = jnp.dot(vis_feats, flat_weight, preferred_element_type=jnp.float32).astype(jnp.bfloat16)
    visual_qkv = visual_qkv.reshape(VIS_ROWS, 3, inner_width)
    picked = visual_qkv[jnp.maximum(vis_src, 0)]
    all_qkv = jnp.where((vis_src >= 0)[:, None, None], picked, text_qkv)
    block_count = SEQUENCE_TOKENS // S_DEV
    qkv_blocks = all_qkv.reshape(block_count, S_DEV, 3, HEAD_TOTAL, HD)
    decay_blocks = log_decay.reshape(HEAD_TOTAL, block_count, S_DEV).transpose(1, 0, 2)
    causal = jnp.arange(S_DEV)[:, None] >= jnp.arange(S_DEV)[None, :]

    def block_step(state_now, block_items):
        block_rows, decay_rows = block_items
        query_rows = block_rows[:, 0].astype(jnp.float32)
        key_rows = block_rows[:, 1].astype(jnp.float32)
        value_rows = block_rows[:, 2].astype(jnp.float32)
        cumulative = jnp.cumsum(decay_rows, axis=1)
        scores = jnp.einsum('shd,thd->hst', query_rows, key_rows, precision=highest)
        decay_gap = jnp.where(causal[None], cumulative[:, :, None] - cumulative[:, None, :], -jnp.inf)
        weights = lax.optimization_barrier((scores * jnp.exp(decay_gap)).astype(jnp.bfloat16)).astype(jnp.float32)
        within = jnp.einsum('hst,thd->shd', weights, value_rows, precision=highest)
        from_state = jnp.exp(cumulative).T[:, :, None] * jnp.einsum('shd,hde->she', query_rows, state_now, precision=highest)
        block_total = cumulative[:, -1]
        scaled_keys = key_rows * jnp.exp(block_total[:, None] - cumulative).T[:, :, None]
        new_state = jnp.exp(block_total)[:, None, None] * state_now + jnp.einsum('thd,the->hde', scaled_keys, value_rows, precision=highest)
        return (new_state, (within + from_state).reshape(S_DEV, inner_width))
    initial = jnp.zeros((HEAD_TOTAL, HD, HD), jnp.float32)
    _, mixed_out = lax.scan(block_step, initial, (qkv_blocks, decay_blocks))
    mixed_out = mixed_out.reshape(SEQUENCE_TOKENS, inner_width)
    mean_square = lax.optimization_barrier(jnp.mean(mixed_out * mixed_out, axis=1, keepdims=True))
    return (mixed_out * lax.rsqrt(mean_square + 1e-05) * norm_gain).astype(jnp.bfloat16)
```

```python
import functools

import jax
import jax.numpy as jnp
from jax import lax
from jax.experimental import pallas as pl
from jax.experimental.pallas import tpu as pltpu
from jax.sharding import PartitionSpec as P

MESH = pl.DeviceIdType.MESH
F32, BF16 = jnp.float32, jnp.bfloat16
NY = 8
FAR = -1e30
T = 128
TOT_Y, STATE_Y, FEAT_Z, TAB_Y, TOT_Z, FEAT_Y, FEAT_X, FEAT_C, TAB_Z, STATE_Z, BACK_Z, BACK_Y, NORM = range(13)


def dot(a, b, dims=((1,), (0,))):
    return lax.dot_general(a, b, (dims, ((), ())), preferred_element_type=F32)


def lanes(h):
    start = h * T if isinstance(h, int) else pl.multiple_of(h * T, T)
    return pl.ds(start, T)


def kernel(
    nz, nh, heads_total,
    text, feats, w_hbm, vis_src, log_decay, gain, out,
    w, zbuf, x48, fbuf, qkv_vis, qkv, s_out, s_in, e_out, e_in, pstate, t_out, t_in, r_out, r_in,
    tot, tot_z, pre, tab, tab_z, weight, cum, mixed, part, norm, send, recv, w_sem,
):
    nx = nh // 2
    vr = qkv_vis.shape[1]
    zrows = 4 * nz
    owners = t_out.shape[0]
    block_cols = fbuf.shape[3]
    me, hd = lax.axis_index("ctx"), lax.axis_index("head")
    z, y = me // NY, me % NY
    x, core = hd // 2, hd % 2

    def y_dev(to):
        return {"ctx": z * NY + to, "head": hd}

    def z_dev(to):
        return {"ctx": to * NY + y, "head": hd}

    def h_dev(to):
        return {"ctx": me, "head": to}

    def put(src, dst, phase, device):
        pltpu.make_async_remote_copy(
            src_ref=src, dst_ref=dst, send_sem=send.at[phase], recv_sem=recv.at[phase],
            device_id=device, device_id_type=MESH,
        ).start()

    def wait(ref, sem):
        pltpu.make_async_copy(ref, ref, sem).wait()

    def y_peers():
        return [lax.rem(y + k, NY) for k in (4, 3, 5, 2, 6, 1, 7)]

    def z_peers():
        return [lax.rem(z + k, nz) for k in range(1, nz)]

    w_copy = pltpu.make_async_copy(w_hbm, w, w_sem)
    w_copy.start()
    barrier = pltpu.get_barrier_semaphore()
    for to in y_peers():
        pl.semaphore_signal(barrier, inc=1, device_id=y_dev(to), device_id_type=MESH)
    for to in z_peers():
        pl.semaphore_signal(barrier, inc=1, device_id=z_dev(to), device_id_type=MESH)
    for k in range(1, nh):
        pl.semaphore_signal(barrier, inc=1, device_id=h_dev(lax.rem(hd + k, nh)), device_id_type=MESH)

    lane = lax.broadcasted_iota(jnp.int32, (NY, T), 1)
    running = log_decay[...]
    step = 1
    while step < T:
        running = running + jnp.where(lane >= step, pltpu.roll(running, step, 1), 0.0)
        step *= 2
    cum[...] = running
    total = jnp.sum(jnp.where(lane == T - 1, running, 0.0), axis=1, keepdims=True)
    total = jnp.broadcast_to(total, (NY, T))
    tot[y] = total

    source_row = jnp.broadcast_to(vis_src[...], (T, T)).astype(F32)
    source = source_row.T
    is_vis = source >= 0.0
    col = lax.broadcasted_iota(jnp.int32, (1, vr), 1)
    col_y = jnp.zeros((1, vr), jnp.int32)
    for k in range(1, NY):
        col_y = col_y + jnp.where(col >= k * zrows, 1, 0)
    col_z = lax.shift_right_logical(col - col_y * zrows, 2)
    row_id = ((col_z * NY + col_y) * 4 + (col & 3)).astype(F32)
    pick = jnp.concatenate(
        [jnp.where(source == row_id[:, j:j + T], 1.0, 0.0) for j in range(0, vr, T)], axis=1
    ).astype(BF16)

    def head_state(h):
        row = jnp.broadcast_to(cum[pl.ds(h, 1), :], (T, T))
        last = jnp.broadcast_to(tot[y, pl.ds(h, 1), :], (T, T))
        tail = jnp.where(is_vis, 0.0, jnp.exp(last - row.T))
        value = text[2, :, lanes(h)].astype(F32) * tail
        high = value.astype(BF16)
        low = (value - high.astype(F32)).astype(BF16)
        both = dot(text[1, :, lanes(h)], jnp.concatenate([high, low], axis=1), ((0,), (0,)))
        s_out[h] = (both[:, :T] + both[:, T:]).astype(BF16)

    for h in range(NY):
        head_state(h)

    own = feats[...].astype(F32)
    quarter = own.shape[1] // 4
    zbuf[z] = jnp.concatenate([own[:, c * quarter:(c + 1) * quarter] for c in range(4)], axis=0).astype(BF16)

    pl.semaphore_wait(barrier, NY - 1 + nz - 1 + nh - 1)

    for to in y_peers():
        put(tot.at[y], tot.at[y], TOT_Y, y_dev(to))
    for to in y_peers():
        put(s_out.at[to], s_in.at[y], STATE_Y, y_dev(to))
    for to in z_peers():
        put(zbuf.at[z], zbuf.at[z], FEAT_Z, z_dev(to))

    tail = total - running
    high = tail.astype(BF16).astype(F32)
    mid = (tail - high).astype(BF16).astype(F32)
    low = tail - high - mid
    pieces = jnp.concatenate([high, mid, low, jnp.ones_like(tail)], axis=0).astype(BF16)
    table = dot(pieces, pick)
    here = table[3 * NY:] > 0.5
    tab[y] = jnp.where(here, table[:NY] + table[NY:2 * NY] + table[2 * NY:3 * NY], FAR)
    for to in y_peers():
        put(tab.at[y], tab.at[y], TAB_Y, y_dev(to))

    s_in[y] = s_out[y]

    wait(tot.at[pl.ds(0, NY - 1)], recv.at[TOT_Y])
    before = jnp.zeros((NY, T), F32)
    for k in range(NY):
        pre[k] = before
        before = before + tot[k]
    tot_z[z] = before
    for to in z_peers():
        put(tot_z.at[z], tot_z.at[z], TOT_Z, z_dev(to))

    wait(zbuf.at[pl.ds(0, nz - 1)], recv.at[FEAT_Z])
    rows = lax.broadcasted_iota(jnp.int32, (256, 16 * nz), 0)
    folded = lax.broadcasted_iota(jnp.int32, (256, 16 * nz), 1)
    wanted = (lax.shift_right_logical(rows, 2) & 15) * 16 + lax.shift_right_logical(rows, 6) * 4 + (rows & 3)
    unfold = jnp.where(wanted == folded, 1.0, 0.0).astype(BF16)
    unfolded = dot(unfold, zbuf[...].reshape(16 * nz, quarter)).astype(BF16)
    for c in range(4):
        x48[:, c * quarter:(c + 1) * quarter] = unfolded[c * 64:c * 64 + zrows]
    fbuf[hd, y] = x48[:, pl.ds(pl.multiple_of(hd * block_cols, T), block_cols)]
    for to in y_peers():
        put(fbuf.at[hd, y], fbuf.at[hd, y], FEAT_Y, y_dev(to))

    wait(s_in.at[pl.ds(0, NY - 1)], recv.at[STATE_Y])
    state = jnp.zeros((T, T), F32)
    for k in range(NY):
        pstate[k] = state
        state = state * jnp.exp(tot[k, pl.ds(y, 1), :]) + s_in[k].astype(F32)
    share = T // owners
    for i in range(owners):
        t_out[i] = state[i * share:(i + 1) * share]
    for i in range(owners):
        @pl.when(z != i)
        def _():
            put(t_out.at[i], t_in.at[z], STATE_Z, z_dev(i))

    wait(tab.at[pl.ds(0, NY - 1)], recv.at[TAB_Y])

    def wide(a):
        return jnp.concatenate([a] * (vr // T), axis=1)

    row_tab = jnp.full((NY, vr), FAR, F32)
    own_tab = jnp.full((NY, vr), FAR, F32)
    for k in range(NY):
        now = tab[k]
        shift = wide(tot[k])
        row_tab = jnp.maximum(row_tab + shift, now)
        own_tab = jnp.where(k < y, jnp.maximum(own_tab + shift, now), own_tab)
    tab_z[z] = row_tab
    for to in z_peers():
        put(tab_z.at[z], tab_z.at[z], TAB_Z, z_dev(to))

    wait(fbuf.at[0, pl.ds(0, NY - 1)], recv.at[FEAT_Y])
    for k in range(1, nx):
        put(fbuf.at[hd], fbuf.at[hd], FEAT_X, h_dev(lax.rem(x + k, nx) * 2 + core))
    put(fbuf.at[hd], fbuf.at[hd], FEAT_C, h_dev(x * 2 + 1 - core))

    wait(tot_z.at[pl.ds(0, nz - 1)], recv.at[TOT_Z])

    @pl.when(z < owners)
    def _():
        wait(t_in.at[pl.ds(0, nz - 1)], recv.at[STATE_Z])
        t_in[z] = t_out[z]
        carry = jnp.zeros((share, T), F32)
        for k in range(nz):
            r_out[k] = carry
            carry = carry * jnp.exp(tot_z[k, pl.ds(y, 1), :]) + t_in[k]
        for to in z_peers():
            put(r_out.at[to], r_in.at[z], BACK_Z, z_dev(to))
        r_in[z] = r_out[z]

    if nx > 1:
        wait(fbuf.at[pl.ds(0, nx - 1)], recv.at[FEAT_X])
        for k in range(1, nx):
            slab = fbuf.at[lax.rem(x + k, nx) * 2 + core]
            put(slab, slab, FEAT_C, h_dev(x * 2 + 1 - core))

    @pl.when(z < owners)
    def _():
        wait(r_in.at[pl.ds(0, owners - 1)], recv.at[BACK_Z])

    @pl.when(z >= owners)
    def _():
        wait(r_in, recv.at[BACK_Z])

    entering = r_in[...].reshape(T, T)
    for to in y_peers():
        e_out[to] = (pstate[to] + entering * jnp.exp(pre[to, pl.ds(y, 1), :])).astype(BF16)
        put(e_out.at[to], e_in.at[y], BACK_Y, y_dev(to))
    e_in[y] = (pstate[y] + entering * jnp.exp(pre[y, pl.ds(y, 1), :])).astype(BF16)

    wait(tab_z.at[pl.ds(0, nz - 1)], recv.at[TAB_Z])
    far_tab = jnp.full((NY, vr), FAR, F32)
    for k in range(nz):
        far_tab = jnp.where(k < z, jnp.maximum(far_tab + wide(tot_z[k]), tab_z[k]), far_tab)
    weight[...] = jnp.exp(jnp.maximum(far_tab + wide(pre[y]), own_tab))

    wait(fbuf.at[pl.ds(0, nx)], recv.at[FEAT_C])
    w_copy.wait()
    everything = jnp.concatenate([fbuf[k].reshape(vr, block_cols) for k in range(nh)], axis=1)
    chunk = 512
    inner = w.shape[2]

    def project(i, _):
        member, part_of = i // (inner // chunk), i % (inner // chunk)
        cols = pl.ds(pl.multiple_of(part_of * chunk, chunk), chunk)
        qkv_vis[member, :, cols] = dot(everything, w[member, :, cols]).astype(BF16)
        return 0

    lax.fori_loop(0, 3 * (inner // chunk), project, 0)

    causal = lax.broadcasted_iota(jnp.int32, (T, T), 0) >= lax.broadcasted_iota(jnp.int32, (T, T), 1)

    def head_within(h):
        at = lanes(h)
        members = []
        for m in range(3):
            placed = dot(pick, qkv_vis[m, :, at])
            members.append(jnp.where(is_vis, placed, text[m, :, at].astype(F32)).astype(BF16))
        query, key, value = members
        qkv[:, at] = query
        row = jnp.broadcast_to(cum[pl.ds(h, 1), :], (T, T))
        gap = row.T - row
        scores = dot(query, key, ((1,), (1,)))
        weights = jnp.where(causal, scores * jnp.exp(jnp.where(causal, gap, 0.0)), 0.0).astype(BF16)
        mixed[:, at] = dot(weights, value)
        visual = dot(query, qkv_vis[1, :, at], ((1,), (1,))) * weight[pl.ds(h, 1), :]
        part[:, at] = dot(visual.astype(BF16), qkv_vis[2, :, at])

    for h in range(NY):
        head_within(h)

    wait(e_in.at[pl.ds(0, NY - 1)], recv.at[BACK_Y])
    squares = jnp.zeros((T, T), F32)
    for h in range(NY):
        at = lanes(h)
        grown = jnp.exp(jnp.broadcast_to(cum[pl.ds(h, 1), :], (T, T)).T)
        result = mixed[:, at] + grown * (dot(qkv[:, at], e_in[h]) + part[:, at])
        mixed[:, at] = result
        squares = squares + result * result

    norm[hd] = jnp.broadcast_to(jnp.sum(squares.T, axis=0, keepdims=True), (8, T))
    for k in range(1, nh):
        put(norm.at[hd], norm.at[hd], NORM, h_dev(lax.rem(hd + k, nh)))
    wait(norm.at[pl.ds(0, nh - 1)], recv.at[NORM])
    square_sum = norm[0]
    for k in range(1, nh):
        square_sum = square_sum + norm[k]
    inverse = lax.rsqrt(square_sum * (1.0 / heads_total) + 1e-05)
    scale = jnp.broadcast_to(inverse[:1], (T, T)).T
    for h in range(NY):
        at = lanes(h)
        out[:, at] = (mixed[:, at] * scale * gain[:, at]).astype(BF16)

    wait(tot.at[pl.ds(0, NY - 1)], send.at[TOT_Y])
    wait(s_in.at[pl.ds(0, NY - 1)], send.at[STATE_Y])
    wait(zbuf.at[pl.ds(0, nz - 1)], send.at[FEAT_Z])
    wait(tab.at[pl.ds(0, NY - 1)], send.at[TAB_Y])
    wait(tot_z.at[pl.ds(0, nz - 1)], send.at[TOT_Z])
    wait(fbuf.at[0, pl.ds(0, NY - 1)], send.at[FEAT_Y])
    if nx > 1:
        wait(fbuf.at[pl.ds(0, nx - 1)], send.at[FEAT_X])
    wait(fbuf.at[pl.ds(0, nx)], send.at[FEAT_C])
    wait(tab_z.at[pl.ds(0, nz - 1)], send.at[TAB_Z])

    @pl.when(z < owners)
    def _():
        wait(t_out.at[pl.ds(0, owners - 1)], send.at[STATE_Z])
        wait(r_out.at[pl.ds(0, nz - 1)], send.at[BACK_Z])

    @pl.when(z >= owners)
    def _():
        wait(t_out, send.at[STATE_Z])

    wait(e_out.at[pl.ds(0, NY - 1)], send.at[BACK_Y])
    wait(norm.at[pl.ds(0, nh - 1)], send.at[NORM])


def local(nz, nh, text_qkv, vis_feats, w_visual, vis_src, log_decay, norm_gain):
    row_count, _, inner = text_qkv.shape
    width = vis_feats.shape[1]
    vr = vis_feats.shape[0] * NY * nz
    owners = 8 if nz >= 8 else nz
    share = T // owners
    vmem = pl.BlockSpec(memory_space=pltpu.VMEM)
    scratch = [
        pltpu.VMEM((3, width, inner), BF16),
        pltpu.VMEM((nz, 16, width // 4), BF16),
        pltpu.VMEM((4 * nz, width), BF16),
        pltpu.VMEM((nh, NY, 4 * nz, width // nh), BF16),
        pltpu.VMEM((3, vr, inner), BF16),
        pltpu.VMEM((row_count, inner), BF16),
        pltpu.VMEM((NY, T, T), BF16),
        pltpu.VMEM((NY, T, T), BF16),
        pltpu.VMEM((NY, T, T), BF16),
        pltpu.VMEM((NY, T, T), BF16),
        pltpu.VMEM((NY, T, T), F32),
        pltpu.VMEM((owners, share, T), F32),
        pltpu.VMEM((nz, share, T), F32),
        pltpu.VMEM((nz, share, T), F32),
        pltpu.VMEM((owners, share, T), F32),
        pltpu.VMEM((NY, NY, T), F32),
        pltpu.VMEM((nz, NY, T), F32),
        pltpu.VMEM((NY, NY, T), F32),
        pltpu.VMEM((NY, NY, vr), F32),
        pltpu.VMEM((nz, NY, vr), F32),
        pltpu.VMEM((NY, vr), F32),
        pltpu.VMEM((NY, T), F32),
        pltpu.VMEM((row_count, inner), F32),
        pltpu.VMEM((row_count, inner), F32),
        pltpu.VMEM((nh, 8, T), F32),
        pltpu.SemaphoreType.DMA((13,)),
        pltpu.SemaphoreType.DMA((13,)),
        pltpu.SemaphoreType.DMA,
    ]
    return pl.pallas_call(
        functools.partial(kernel, nz, nh, inner * nh),
        out_shape=jax.ShapeDtypeStruct((row_count, inner), BF16),
        in_specs=[vmem, vmem, pl.BlockSpec(memory_space=pl.ANY), vmem, vmem, vmem],
        out_specs=vmem,
        scratch_shapes=scratch,
        compiler_params=pltpu.CompilerParams(
            collective_id=0, has_side_effects=True, vmem_limit_bytes=48 * 1024 * 1024
        ),
        name="lightning",
    )(
        text_qkv.transpose(1, 0, 2),
        vis_feats,
        w_visual.transpose(1, 0, 2),
        vis_src.reshape(1, row_count),
        log_decay,
        norm_gain.reshape(1, inner),
    )


def solution(mesh):
    placed = (
        P("ctx", None, "head"),
        P("ctx", None),
        P(None, None, "head"),
        P("ctx"),
        P("head", "ctx"),
        P("head"),
    )
    nz, nh = mesh.shape["ctx"] // NY, mesh.shape["head"]
    return jax.shard_map(
        functools.partial(local, nz, nh), mesh=mesh, in_specs=placed, out_specs=P("ctx", "head"), check_vma=False
    )
```

```python
import functools

import jax
import jax.numpy as jnp
from jax import lax
from jax.experimental import pallas as pl
from jax.experimental.pallas import tpu as pltpu
from jax.sharding import PartitionSpec as P

MESH = pl.DeviceIdType.MESH
F32, BF16 = jnp.float32, jnp.bfloat16
NY = 8
FAR = -1e30
T = 128
TOT_Y, RAW_Y, FEAT_Y, TOT_Z, FEAT_X, FEAT_C, STATE_Z, BACK_Y, NORM, FEAT_Z, TAB_Z, BACK_Z, STATE_Y = range(13)
RINGS = {FEAT_Z: 16, TAB_Z: 32, BACK_Z: 48, STATE_Y: 64}
RECEIVES = 72


def halves(nz):
    half = nz // 2
    return (half, 4, 1) if half >= 6 else (half, half, 0)


def dot(a, b, dims=((1,), (0,))):
    return lax.dot_general(a, b, (dims, ((), ())), preferred_element_type=F32)


def lanes(h):
    start = h * T if isinstance(h, int) else pl.multiple_of(h * T, T)
    return pl.ds(start, T)


def kernel(
    nz, nh, heads_total,
    text_in, feats_in, w_in, vis_src_in, log_decay_in, gain_in, out,
    text, feats, w, vis_src, log_decay, gain, ybuf, fbuf, kv_sum, query_sum, kv_vis, query_all, s_out, s_in, e_out, e_in, pstate,
    t_out, t_in, r_out, r_in, raw, tot, tot_z, pre, tab_z, weight, decay, grown, mixed, part, norm,
    send, recv, load,
):
    nx = nh // 2
    vr = kv_vis.shape[1]
    yrows = 4 * NY
    half, owners, first = halves(nz)
    share = T // owners
    block_cols = fbuf.shape[3]
    inner = w.shape[2]
    me, hd = lax.axis_index("ctx"), lax.axis_index("head")
    z, y = me // NY, me % NY
    x, core = hd // 2, hd % 2
    base = z // half * half
    slot = z - base - first
    is_owner = (slot >= 0) & (slot < owners)
    block = core * nx + x

    def y_dev(to):
        return {"ctx": z * NY + to, "head": hd}

    def z_dev(to):
        return {"ctx": to * NY + y, "head": hd}

    def h_dev(to):
        return {"ctx": me, "head": to}

    leaving, arriving = [], []

    def put(src, dst, phase, device, receive=None):
        pltpu.make_async_remote_copy(
            src_ref=src, dst_ref=dst, send_sem=send.at[phase], recv_sem=recv.at[phase if receive is None else receive],
            device_id=device, device_id_type=MESH,
        ).start()

    def wait(ref, sem):
        pltpu.make_async_copy(ref, ref, sem).wait()

    def expect(phase, ref_out, ref_in):
        leaving.append(lambda: wait(ref_out, send.at[phase]))
        arriving.append((phase, lambda: wait(ref_in, recv.at[phase])))

    def arrived(phase):
        (entry,) = [e for e in arriving if e[0] == phase]
        arriving.remove(entry)
        entry[1]()

    def finish():
        for _, waiting in arriving + [(None, e) for e in leaving]:
            waiting()

    def y_peers():
        return [lax.rem(y + k, NY) for k in (4, 3, 5, 2, 6, 1, 7)]

    def z_peers():
        return [lax.rem(z + k, nz) for k in sorted(range(1, nz), key=lambda k: -min(k, nz - k))]

    def near(k, here, count):
        return lax.rem(here + (k % 2 * 2 - 1) * ((k + 1) // 2) + count, count)

    barrier = pltpu.get_barrier_semaphore()
    for to in y_peers():
        pl.semaphore_signal(barrier, inc=1, device_id=y_dev(to), device_id_type=MESH)
    for to in z_peers():
        pl.semaphore_signal(barrier, inc=1, device_id=z_dev(to), device_id_type=MESH)
    for k in range(1, nh):
        pl.semaphore_signal(barrier, inc=1, device_id=h_dev(lax.rem(hd + k, nh)), device_id_type=MESH)

    pairs = [(feats_in, feats), (log_decay_in, log_decay), (vis_src_in, vis_src), (text_in.at[2], text.at[2]),
             (text_in.at[1], text.at[1]), (text_in.at[0], text.at[0]), (gain_in, gain), (w_in, w)]
    loads = [pltpu.make_async_copy(src, dst, load.at[i]) for i, (src, dst) in enumerate(pairs)]
    for copy in loads:
        copy.start()

    loads[0].wait()
    quarters = [
        feats[:, pl.ds(pl.multiple_of((core * nx + c) * block_cols, T), block_cols)].astype(F32) for c in range(nx)
    ]
    ybuf[y] = jnp.concatenate(quarters, axis=0).astype(BF16)

    pl.semaphore_wait(barrier, NY - 1 + nz - 1 + nh - 1)
    for to in y_peers():
        put(ybuf.at[y], ybuf.at[y], FEAT_Y, y_dev(to))
    expect(FEAT_Y, ybuf.at[pl.ds(0, NY - 1)], ybuf.at[pl.ds(0, NY - 1)])

    loads[1].wait()
    lane = lax.broadcasted_iota(jnp.int32, (NY, T), 1)
    running = log_decay[...]
    step = 1
    while step < T:
        running = running + jnp.where(lane >= step, pltpu.roll(running, step, 1), 0.0)
        step *= 2

    def last_of(a):
        last = jnp.sum(jnp.where(lane == T - 1, a, 0.0), axis=1, keepdims=True)
        return jnp.broadcast_to(last, (NY, T))

    tot[y] = last_of(running)
    for to in y_peers():
        put(tot.at[y], tot.at[y], TOT_Y, y_dev(to))
    expect(TOT_Y, tot.at[pl.ds(0, NY - 1)], tot.at[pl.ds(0, NY - 1)])

    loads[2].wait()
    source_row = jnp.broadcast_to(vis_src[...], (T, T)).astype(F32)
    raw[y] = jnp.concatenate([running, source_row[:NY]], axis=0)
    source = source_row.T
    is_vis = source >= 0.0
    loads[3].wait()
    loads[4].wait()

    def head_state(h):
        row = jnp.broadcast_to(raw[y, pl.ds(h, 1), :], (T, T))
        last = jnp.broadcast_to(tot[y, pl.ds(h, 1), :], (T, T))
        tail = jnp.where(is_vis, 0.0, jnp.exp(last - row.T))
        value = text[2, :, lanes(h)].astype(F32) * tail
        high = value.astype(BF16)
        low = (value - high.astype(F32)).astype(BF16)
        both = dot(text[1, :, lanes(h)], jnp.concatenate([high, low], axis=1), ((0,), (0,)))
        s_out[h] = (both[:, :T] + both[:, T:]).astype(BF16)

    for h in range(NY):
        head_state(h)

    for p in range(owners):
        at = pl.ds(p * share, share)
        for to in y_peers():
            put(s_out.at[to, at], s_in.at[y, at], STATE_Y, y_dev(to), RINGS[STATE_Y] + p)
    leaving.append(lambda: wait(s_out.at[pl.ds(0, NY - 1)], send.at[STATE_Y]))
    for to in y_peers():
        put(raw.at[y], raw.at[y], RAW_Y, y_dev(to))
    expect(RAW_Y, raw.at[pl.ds(0, NY - 1)], raw.at[pl.ds(0, NY - 1)])
    s_in[y] = s_out[y]

    row_id = lax.broadcasted_iota(jnp.int32, (1, vr), 1).astype(F32)

    def one_hot(column):
        return jnp.concatenate(
            [jnp.where(column == row_id[:, j:j + T], 1.0, 0.0) for j in range(0, vr, T)], axis=1
        ).astype(BF16)

    pick = one_hot(source)

    arrived(FEAT_Y)
    rows = lax.broadcasted_iota(jnp.int32, (yrows, 4 * nx * NY), 0)
    folded = lax.broadcasted_iota(jnp.int32, (yrows, 4 * nx * NY), 1)
    wanted = lax.shift_right_logical(rows, 2) * (4 * nx) + x * 4 + (rows & 3)
    unfold = jnp.where(wanted == folded, 1.0, 0.0).astype(BF16)
    fbuf[block, z] = dot(unfold, ybuf[...].reshape(4 * nx * NY, block_cols)).astype(BF16)
    for to in z_peers():
        put(fbuf.at[block, z], fbuf.at[block, z], FEAT_Z, z_dev(to), RINGS[FEAT_Z] + z)
    leaving.append(lambda: wait(fbuf.at[0, pl.ds(0, nz - 1)], send.at[FEAT_Z]))

    arrived(TOT_Y)
    before = jnp.zeros((NY, T), F32)
    for k in range(NY):
        pre[k] = before
        before = before + tot[k]
    tot_z[z] = before
    for to in z_peers():
        put(tot_z.at[z], tot_z.at[z], TOT_Z, z_dev(to))
    expect(TOT_Z, tot_z.at[pl.ds(0, nz - 1)], tot_z.at[pl.ds(0, nz - 1)])

    causal = lax.broadcasted_iota(jnp.int32, (T, T), 0) >= lax.broadcasted_iota(jnp.int32, (T, T), 1)

    def head_decay(h):
        row = jnp.broadcast_to(raw[y, pl.ds(h, 1), :], (T, T))
        col = row.T
        grown[h] = jnp.exp(col)
        decay[h] = jnp.where(causal, jnp.exp(jnp.where(causal, col - row, 0.0)), 0.0)

    for h in range(NY):
        head_decay(h)

    def forward(k, _):
        piece = fbuf.at[block, near(k, z, nz)]

        @pl.when(k > 0)
        def _():
            wait(piece, recv.at[RINGS[FEAT_Z] + near(k, z, nz)])

        for j in range(1, nx):
            put(piece, piece, FEAT_X, h_dev(lax.rem(x + j, nx) * 2 + core))
        put(piece, piece, FEAT_C, h_dev(x * 2 + 1 - core))
        return 0

    early = nz // 2 + 1
    for p in range(owners):
        at = pl.ds(p * share, share)
        wait(s_in.at[pl.ds(0, NY - 1), at], recv.at[RINGS[STATE_Y] + p])
        state = jnp.zeros((share, T), F32)
        for k in range(NY):
            pstate[k, at] = state
            state = state * jnp.exp(tot[k, pl.ds(y, 1), :]) + s_in[k, at].astype(F32)
        t_out[p] = state
        for begin, last in ((0, half - 2), (half, nz - 2)):
            owner = begin + first + p

            @pl.when((z != owner) & (z <= last))
            def _():
                put(t_out.at[p], t_in.at[z], STATE_Z, z_dev(owner))

    def state_z_left():
        for k in range(nz):
            targets = [
                begin + first + p for begin, last in ((0, half - 2), (half, nz - 2)) if k <= last for p in range(owners)
                if begin + first + p != k
            ]

            @pl.when(z == k)
            def _():
                if targets:
                    wait(t_in.at[pl.ds(0, len(targets))], send.at[STATE_Z])

    def state_z_here():
        for k in range(nz):
            begin = k // half * half
            sources = [i for i in range(nz) if i <= begin + half - 2 and i != k]

            @pl.when((z == k) & is_owner)
            def _():
                if sources:
                    wait(t_in.at[pl.ds(0, len(sources))], recv.at[STATE_Z])

    leaving.append(state_z_left)
    arriving.append((STATE_Z, state_z_here))

    lax.fori_loop(0, early, forward, 0)

    arrived(RAW_Y)
    to_end, to_own = [None] * NY, [None] * NY
    after, after_own = jnp.zeros((NY, T), F32), jnp.zeros((NY, T), F32)
    for k in reversed(range(NY)):
        rest = tot[k] - raw[k, :NY]
        mine = jnp.full((NY, T), k, jnp.int32) < y
        to_end[k] = rest + after
        to_own[k] = jnp.where(mine, rest + after_own, 0.0)
        after = after + tot[k]
        after_own = after_own + jnp.where(mine, tot[k], 0.0)
    pieces = []
    for group in (to_end, to_own):
        logs = jnp.concatenate(group, axis=1)
        high = logs.astype(BF16).astype(F32)
        mid = (logs - high).astype(BF16).astype(F32)
        pieces += [high, mid, logs - high - mid]
    reach = lax.broadcasted_iota(jnp.int32, (NY, NY * T), 1) < y * T
    pieces += [jnp.ones((NY, NY * T), F32), jnp.where(reach, 1.0, 0.0)]
    hot = jnp.concatenate(
        [one_hot(jnp.broadcast_to(raw[k, pl.ds(NY, 1), :], (T, T)).T) for k in range(NY)], axis=0
    )
    table = dot(jnp.concatenate(pieces, axis=0).astype(BF16), hot)
    table = [table[i * NY:(i + 1) * NY] for i in range(8)]
    row_tab = jnp.where(table[6] > 0.5, table[0] + table[1] + table[2], FAR)
    own_tab = jnp.where(table[7] > 0.5, table[3] + table[4] + table[5], FAR)
    tab_z[z] = row_tab
    for to in z_peers():
        @pl.when(to > z)
        def _():
            put(tab_z.at[z], tab_z.at[z], TAB_Z, z_dev(to), RINGS[TAB_Z] + z)

    def tab_z_left():
        for k in range(nz):
            @pl.when(z == k)
            def _():
                if k < nz - 1:
                    wait(tab_z.at[pl.ds(0, nz - 1 - k)], send.at[TAB_Z])

    leaving.append(tab_z_left)

    def wide(a):
        return jnp.concatenate([a] * (vr // T), axis=1)

    lax.fori_loop(early, nz, forward, 0)
    slabs = fbuf.at[pl.ds(0, nx - 1)]
    expect(FEAT_X, slabs, slabs)

    arrived(TOT_Z)
    arrived(STATE_Z)

    @pl.when(is_owner)
    def _():
        t_in[z] = t_out[slot]

    for begin in (0, half):
        @pl.when(is_owner & (base == begin))
        def _():
            carry = jnp.zeros((share, T), F32)
            for k in range(begin + half):
                if k >= begin:
                    r_out[k] = carry
                if k < begin + half - 1:
                    carry = carry * jnp.exp(tot_z[k, pl.ds(y, 1), :]) + t_in[k]
            for k in range(max(begin, 1), begin + half):
                @pl.when(z != k)
                def _():
                    put(r_out.at[k], r_in.at[slot], BACK_Z, z_dev(k), RINGS[BACK_Z] + slot)

    @pl.when(is_owner)
    def _():
        r_in[slot] = r_out[z]

    @pl.when(z == 0)
    def _():
        r_in[...] = jnp.zeros_like(r_in)

    def back_z_left():
        for k in range(nz):
            begin = k // half * half
            targets = [i for i in range(max(begin, 1), begin + half) if i != k]

            @pl.when((z == k) & is_owner)
            def _():
                if targets:
                    wait(r_out.at[pl.ds(0, len(targets))], send.at[BACK_Z])

    leaving.append(back_z_left)

    arrived(FEAT_X)
    for j in range(1, nx):
        slab = fbuf.at[core * nx + lax.rem(x + j, nx)]
        put(slab, slab, FEAT_C, h_dev(x * 2 + 1 - core))
    expect(FEAT_C, fbuf.at[pl.ds(0, nx)], fbuf.at[pl.ds(0, nx)])

    for copy in loads[5:]:
        copy.wait()
    chunk = 256

    def feature_half(side):
        columns = [fbuf[side * nx + j].reshape(vr, block_cols) for j in range(nx)]
        size = nx * block_cols
        return jnp.concatenate(columns, axis=1), pl.ds(pl.multiple_of(side * size, size), size)

    near_side, near_rows = feature_half(core)
    for m in range(2):
        for start in range(0, inner, chunk):
            cols = pl.ds(start, chunk)
            kv_sum[m, :, cols] = dot(near_side, w[m + 1, near_rows, cols])
    placed = dot(pick, near_side).astype(BF16)
    for start in range(0, inner, chunk):
        cols = pl.ds(start, chunk)
        query_sum[:, cols] = dot(placed, w[0, near_rows, cols])

    def enter(owner, _):
        @pl.when((owner != slot) & (z > 0))
        def _():
            wait(r_in.at[owner], recv.at[RINGS[BACK_Z] + owner])

        at = pl.ds(pl.multiple_of(owner * share, share), share)
        entering = r_in[owner]
        for to in y_peers():
            e_out[to, at] = (pstate[to, at] + entering * jnp.exp(pre[to, pl.ds(y, 1), :])).astype(BF16)
            put(e_out.at[to, at], e_in.at[y, at], BACK_Y, y_dev(to))
        e_in[y, at] = (pstate[y, at] + entering * jnp.exp(pre[y, pl.ds(y, 1), :])).astype(BF16)
        return 0

    lax.fori_loop(0, owners, enter, 0)
    expect(BACK_Y, e_out.at[pl.ds(0, NY - 1)], e_in.at[pl.ds(0, NY - 1)])

    weight[...] = jnp.full((NY, vr), FAR, F32)
    for k in range(nz - 1):
        @pl.when(k < z)
        def _():
            wait(tab_z.at[k], recv.at[RINGS[TAB_Z] + k])
            weight[...] = jnp.maximum(weight[...] + wide(tot_z[k]), tab_z[k])

    weight[...] = jnp.exp(jnp.maximum(weight[...] + wide(pre[y]), own_tab))

    arrived(FEAT_C)
    far_side, far_rows = feature_half(1 - core)
    for m in range(2):
        for start in range(0, inner, chunk):
            cols = pl.ds(start, chunk)
            kv_vis[m, :, cols] = (kv_sum[m, :, cols] + dot(far_side, w[m + 1, far_rows, cols])).astype(BF16)
    placed = dot(pick, far_side).astype(BF16)
    for start in range(0, inner, chunk):
        cols = pl.ds(start, chunk)
        query = (query_sum[:, cols] + dot(placed, w[0, far_rows, cols])).astype(BF16).astype(F32)
        mask = jnp.concatenate([is_vis] * (chunk // T), axis=1)
        query_all[:, cols] = jnp.where(mask, query, text[0, :, cols].astype(F32)).astype(BF16)

    def head_within(h):
        at = lanes(h)
        query = query_all[:, at]
        key, value = [
            jnp.where(is_vis, dot(pick, kv_vis[m, :, at]), text[m + 1, :, at].astype(F32)).astype(BF16) for m in range(2)
        ]
        weights = (dot(query, key, ((1,), (1,))) * decay[h]).astype(BF16)
        mixed[:, at] = dot(weights, value)
        visual = dot(query, kv_vis[0, :, at], ((1,), (1,))) * weight[pl.ds(h, 1), :]
        part[:, at] = dot(visual.astype(BF16), kv_vis[1, :, at])

    for h in range(NY):
        head_within(h)

    arrived(BACK_Y)
    squares = jnp.zeros((T, T), F32)
    for h in range(NY):
        at = lanes(h)
        result = mixed[:, at] + grown[h] * (dot(query_all[:, at], e_in[h]) + part[:, at])
        mixed[:, at] = result
        squares = squares + result * result

    norm[hd] = jnp.broadcast_to(jnp.sum(squares.T, axis=0, keepdims=True), (8, T))
    for k in range(1, nh):
        put(norm.at[hd], norm.at[hd], NORM, h_dev(lax.rem(hd + k, nh)))
    expect(NORM, norm.at[pl.ds(0, nh - 1)], norm.at[pl.ds(0, nh - 1)])
    arrived(NORM)
    square_sum = norm[0]
    for k in range(1, nh):
        square_sum = square_sum + norm[k]
    inverse = lax.rsqrt(square_sum * (1.0 / heads_total) + 1e-05)
    scale = jnp.broadcast_to(inverse[:1], (T, T)).T
    for h in range(NY):
        at = lanes(h)
        out[:, at] = (mixed[:, at] * scale * gain[:, at]).astype(BF16)

    finish()


def hbm(a):
    return pltpu.with_memory_space_constraint(a, pltpu.HBM)


def local(nz, nh, text_qkv, vis_feats, w_visual, vis_src, log_decay, norm_gain):
    row_count, _, inner = text_qkv.shape
    width = vis_feats.shape[1]
    vr = vis_feats.shape[0] * NY * nz
    _, owners, _ = halves(nz)
    share = T // owners
    vmem = pl.BlockSpec(memory_space=pltpu.VMEM)
    anywhere = pl.BlockSpec(memory_space=pltpu.HBM)
    scratch = [
        pltpu.VMEM((3, row_count, inner), BF16),
        pltpu.VMEM(vis_feats.shape, BF16),
        pltpu.VMEM((3, width, inner), BF16),
        pltpu.VMEM((1, row_count), jnp.int32),
        pltpu.VMEM(log_decay.shape, F32),
        pltpu.VMEM((1, inner), F32),
        pltpu.VMEM((NY, 4 * (nh // 2), width // nh), BF16),
        pltpu.VMEM((nh, nz, 4 * NY, width // nh), BF16),
        pltpu.VMEM((2, vr, inner), F32),
        pltpu.VMEM((row_count, inner), F32),
        pltpu.VMEM((2, vr, inner), BF16),
        pltpu.VMEM((row_count, inner), BF16),
        pltpu.VMEM((NY, T, T), BF16),
        pltpu.VMEM((NY, T, T), BF16),
        pltpu.VMEM((NY, T, T), BF16),
        pltpu.VMEM((NY, T, T), BF16),
        pltpu.VMEM((NY, T, T), F32),
        pltpu.VMEM((owners, share, T), F32),
        pltpu.VMEM((nz, share, T), F32),
        pltpu.VMEM((nz, share, T), F32),
        pltpu.VMEM((owners, share, T), F32),
        pltpu.VMEM((NY, 2 * NY, T), F32),
        pltpu.VMEM((NY, NY, T), F32),
        pltpu.VMEM((nz, NY, T), F32),
        pltpu.VMEM((NY, NY, T), F32),
        pltpu.VMEM((nz, NY, vr), F32),
        pltpu.VMEM((NY, vr), F32),
        pltpu.VMEM((NY, T, T), F32),
        pltpu.VMEM((NY, T, T), F32),
        pltpu.VMEM((row_count, inner), F32),
        pltpu.VMEM((row_count, inner), F32),
        pltpu.VMEM((nh, 8, T), F32),
        pltpu.SemaphoreType.DMA((13,)),
        pltpu.SemaphoreType.DMA((RECEIVES,)),
        pltpu.SemaphoreType.DMA((8,)),
    ]
    return pl.pallas_call(
        functools.partial(kernel, nz, nh, inner * nh),
        out_shape=jax.ShapeDtypeStruct((row_count, inner), BF16),
        in_specs=[anywhere] * 6,
        out_specs=vmem,
        scratch_shapes=scratch,
        compiler_params=pltpu.CompilerParams(
            collective_id=0, has_side_effects=True, vmem_limit_bytes=48 * 1024 * 1024
        ),
        name="lightning",
    )(
        hbm(text_qkv.transpose(1, 0, 2)),
        hbm(vis_feats),
        hbm(w_visual.transpose(1, 0, 2)),
        hbm(vis_src.reshape(1, row_count)),
        hbm(log_decay),
        hbm(norm_gain.reshape(1, inner)),
    )


def solution(mesh):
    placed = (
        P("ctx", None, "head"),
        P("ctx", None),
        P(None, None, "head"),
        P("ctx"),
        P("head", "ctx"),
        P("head"),
    )
    nz, nh = mesh.shape["ctx"] // NY, mesh.shape["head"]
    return jax.shard_map(
        functools.partial(local, nz, nh), mesh=mesh, in_specs=placed, out_specs=P("ctx", "head"), check_vma=False
    )
```

```python
import functools

import jax
import jax.numpy as jnp
from jax import lax
from jax.experimental import pallas as pl
from jax.experimental.pallas import tpu as pltpu
from jax.sharding import PartitionSpec as P

MESH = pl.DeviceIdType.MESH
F32, BF16 = jnp.float32, jnp.bfloat16
NY = 8
FAR = -1e30
T = 128
TOT_Y, RAW_Y, FEAT_Y, TOT_Z, FEAT_X, FEAT_C, STATE_Z, BACK_Y, NORM, FEAT_Z, TAB_Z, BACK_Z, STATE_Y = range(13)
RINGS = {FEAT_Z: 16, TAB_Z: 32, BACK_Z: 48, STATE_Y: 64}
RECEIVES = 72


def halves(nz):
    half = nz // 2
    return (half, 4, 1) if half >= 6 else (half, half, 0)


def dot(a, b, dims=((1,), (0,))):
    return lax.dot_general(a, b, (dims, ((), ())), preferred_element_type=F32)


def lanes(h):
    start = h * T if isinstance(h, int) else pl.multiple_of(h * T, T)
    return pl.ds(start, T)


def kernel(
    nz, nh, heads_total,
    text_in, feats_in, w_in, vis_src_in, log_decay_in, gain_in, out,
    text, feats, w, vis_src, log_decay, gain, ybuf, fbuf, kv_sum, query_sum, kv_all, query_all, s_out, s_in, e_out, e_in, pstate,
    t_out, t_in, r_out, r_in, raw, tot, tot_z, pre, tab_z, weight, factor, grown, mixed, norm,
    send, recv, load,
):
    nx = nh // 2
    vr = kv_sum.shape[1]
    yrows = 4 * NY
    half, owners, first = halves(nz)
    share = T // owners
    block_cols = fbuf.shape[3]
    inner = w.shape[2]
    me, hd = lax.axis_index("ctx"), lax.axis_index("head")
    z, y = me // NY, me % NY
    x, core = hd // 2, hd % 2
    base = z // half * half
    slot = z - base - first
    is_owner = (slot >= 0) & (slot < owners)
    block = core * nx + x

    def y_dev(to):
        return {"ctx": z * NY + to, "head": hd}

    def z_dev(to):
        return {"ctx": to * NY + y, "head": hd}

    def h_dev(to):
        return {"ctx": me, "head": to}

    leaving, arriving = [], []

    def put(src, dst, phase, device, receive=None):
        pltpu.make_async_remote_copy(
            src_ref=src, dst_ref=dst, send_sem=send.at[phase], recv_sem=recv.at[phase if receive is None else receive],
            device_id=device, device_id_type=MESH,
        ).start()

    def wait(ref, sem):
        pltpu.make_async_copy(ref, ref, sem).wait()

    def expect(phase, ref_out, ref_in):
        leaving.append(lambda: wait(ref_out, send.at[phase]))
        arriving.append((phase, lambda: wait(ref_in, recv.at[phase])))

    def arrived(phase):
        (entry,) = [e for e in arriving if e[0] == phase]
        arriving.remove(entry)
        entry[1]()

    def finish():
        for _, waiting in arriving + [(None, e) for e in leaving]:
            waiting()

    def y_peers():
        return [lax.rem(y + k, NY) for k in (4, 3, 5, 2, 6, 1, 7)]

    def z_peers():
        return [lax.rem(z + k, nz) for k in sorted(range(1, nz), key=lambda k: -min(k, nz - k))]

    def near(k, here, count):
        return lax.rem(here + (k % 2 * 2 - 1) * ((k + 1) // 2) + count, count)

    barrier = pltpu.get_barrier_semaphore()
    for to in z_peers():
        pl.semaphore_signal(barrier, inc=1, device_id=z_dev(to), device_id_type=MESH)
    for to in y_peers():
        pl.semaphore_signal(barrier, inc=1, device_id=y_dev(to), device_id_type=MESH)
    for k in range(1, nh):
        pl.semaphore_signal(barrier, inc=1, device_id=h_dev(lax.rem(hd + k, nh)), device_id_type=MESH)

    pairs = [(feats_in, feats), (log_decay_in, log_decay), (vis_src_in, vis_src), (text_in.at[2], text.at[2]),
             (text_in.at[1], text.at[1]), (text_in.at[0], text.at[0]), (gain_in, gain), (w_in, w)]
    loads = [pltpu.make_async_copy(src, dst, load.at[i]) for i, (src, dst) in enumerate(pairs)]
    for copy in loads:
        copy.start()

    loads[0].wait()
    quarters = [
        feats[:, pl.ds(pl.multiple_of((core * nx + c) * block_cols, T), block_cols)].astype(F32) for c in range(nx)
    ]
    ybuf[y] = jnp.concatenate(quarters, axis=0).astype(BF16)

    pl.semaphore_wait(barrier, NY - 1 + nz - 1 + nh - 1)
    for to in y_peers():
        put(ybuf.at[y], ybuf.at[y], FEAT_Y, y_dev(to))
    expect(FEAT_Y, ybuf.at[pl.ds(0, NY - 1)], ybuf.at[pl.ds(0, NY - 1)])

    loads[1].wait()
    lane = lax.broadcasted_iota(jnp.int32, (NY, T), 1)
    running = log_decay[...]
    step = 1
    while step < T:
        running = running + jnp.where(lane >= step, pltpu.roll(running, step, 1), 0.0)
        step *= 2

    def last_of(a):
        last = jnp.sum(jnp.where(lane == T - 1, a, 0.0), axis=1, keepdims=True)
        return jnp.broadcast_to(last, (NY, T))

    tot[y] = last_of(running)
    for to in y_peers():
        put(tot.at[y], tot.at[y], TOT_Y, y_dev(to))
    expect(TOT_Y, tot.at[pl.ds(0, NY - 1)], tot.at[pl.ds(0, NY - 1)])

    loads[2].wait()
    source_row = jnp.broadcast_to(vis_src[...], (T, T)).astype(F32)
    raw[y] = jnp.concatenate([running, source_row[:NY]], axis=0)
    source = source_row.T
    is_vis = source >= 0.0
    loads[3].wait()
    loads[4].wait()

    def head_state(h):
        row = jnp.broadcast_to(raw[y, pl.ds(h, 1), :], (T, T))
        last = jnp.broadcast_to(tot[y, pl.ds(h, 1), :], (T, T))
        tail = jnp.where(is_vis, 0.0, jnp.exp(last - row.T))
        value = text[2, :, lanes(h)].astype(F32) * tail
        high = value.astype(BF16)
        low = (value - high.astype(F32)).astype(BF16)
        both = dot(text[1, :, lanes(h)], jnp.concatenate([high, low], axis=1), ((0,), (0,)))
        s_out[h] = (both[:, :T] + both[:, T:]).astype(BF16)

    for h in range(NY):
        head_state(h)

    for p in range(owners):
        at = pl.ds(p * share, share)
        for to in y_peers():
            put(s_out.at[to, at], s_in.at[y, at], STATE_Y, y_dev(to), RINGS[STATE_Y] + p)
    leaving.append(lambda: wait(s_out.at[pl.ds(0, NY - 1)], send.at[STATE_Y]))
    for to in y_peers():
        put(raw.at[y], raw.at[y], RAW_Y, y_dev(to))
    expect(RAW_Y, raw.at[pl.ds(0, NY - 1)], raw.at[pl.ds(0, NY - 1)])
    s_in[y] = s_out[y]

    row_id = lax.broadcasted_iota(jnp.int32, (1, vr), 1).astype(F32)

    def one_hot(column):
        return jnp.concatenate(
            [jnp.where(column == row_id[:, j:j + T], 1.0, 0.0) for j in range(0, vr, T)], axis=1
        ).astype(BF16)

    pick = one_hot(source)

    arrived(FEAT_Y)
    rows = lax.broadcasted_iota(jnp.int32, (yrows, 4 * nx * NY), 0)
    folded = lax.broadcasted_iota(jnp.int32, (yrows, 4 * nx * NY), 1)
    wanted = lax.shift_right_logical(rows, 2) * (4 * nx) + x * 4 + (rows & 3)
    unfold = jnp.where(wanted == folded, 1.0, 0.0).astype(BF16)
    fbuf[block, z] = dot(unfold, ybuf[...].reshape(4 * nx * NY, block_cols)).astype(BF16)
    for to in z_peers():
        put(fbuf.at[block, z], fbuf.at[block, z], FEAT_Z, z_dev(to), RINGS[FEAT_Z] + z)
    leaving.append(lambda: wait(fbuf.at[0, pl.ds(0, nz - 1)], send.at[FEAT_Z]))

    arrived(TOT_Y)
    before = jnp.zeros((NY, T), F32)
    for k in range(NY):
        pre[k] = before
        before = before + tot[k]
    tot_z[z] = before
    for to in z_peers():
        put(tot_z.at[z], tot_z.at[z], TOT_Z, z_dev(to))
    expect(TOT_Z, tot_z.at[pl.ds(0, nz - 1)], tot_z.at[pl.ds(0, nz - 1)])

    def forward(k, _):
        piece = fbuf.at[block, near(k, z, nz)]

        @pl.when(k > 0)
        def _():
            wait(piece, recv.at[RINGS[FEAT_Z] + near(k, z, nz)])

        for j in range(1, nx):
            put(piece, piece, FEAT_X, h_dev(lax.rem(x + j, nx) * 2 + core))
        put(piece, piece, FEAT_C, h_dev(x * 2 + 1 - core))
        return 0

    lax.fori_loop(0, 1, forward, 0)

    causal = lax.broadcasted_iota(jnp.int32, (T, T), 0) >= lax.broadcasted_iota(jnp.int32, (T, T), 1)

    def head_decay(h):
        row = jnp.broadcast_to(raw[y, pl.ds(h, 1), :], (T, T))
        col = row.T
        grown[h] = jnp.exp(col)
        factor[h, :, vr:] = jnp.where(causal, jnp.exp(jnp.where(causal, col - row, 0.0)), 0.0)

    for h in range(NY):
        head_decay(h)

    early = nz // 2 + 1
    for p in range(owners):
        at = pl.ds(p * share, share)
        wait(s_in.at[pl.ds(0, NY - 1), at], recv.at[RINGS[STATE_Y] + p])
        state = jnp.zeros((share, T), F32)
        for k in range(NY):
            pstate[k, at] = state
            state = state * jnp.exp(tot[k, pl.ds(y, 1), :]) + s_in[k, at].astype(F32)
        t_out[p] = state

        @pl.when(z == 0)
        def _():
            put(t_out.at[p], r_in.at[p], BACK_Z, z_dev(1), RINGS[BACK_Z] + p)

        for begin, last in ((0, half - 2), (half, nz - 2)):
            owner = begin + first + p

            @pl.when((z != owner) & (z <= last))
            def _():
                put(t_out.at[p], t_in.at[z], STATE_Z, z_dev(owner))

    def enter(owner, _):
        @pl.when((z == 1) | ((z > 1) & (owner != slot)))
        def _():
            wait(r_in.at[owner], recv.at[RINGS[BACK_Z] + owner])

        at = pl.ds(pl.multiple_of(owner * share, share), share)
        entering = r_in[owner]
        for to in y_peers():
            e_out[to, at] = (pstate[to, at] + entering * jnp.exp(pre[to, pl.ds(y, 1), :])).astype(BF16)
            put(e_out.at[to, at], e_in.at[y, at], BACK_Y, y_dev(to))
        e_in[y, at] = (pstate[y, at] + entering * jnp.exp(pre[y, pl.ds(y, 1), :])).astype(BF16)
        return 0

    @pl.when(z == 0)
    def _():
        r_in[...] = jnp.zeros_like(r_in)
        lax.fori_loop(0, owners, enter, 0)

    def state_z_left():
        for k in range(nz):
            targets = [
                begin + first + p for begin, last in ((0, half - 2), (half, nz - 2)) if k <= last for p in range(owners)
                if begin + first + p != k
            ]

            @pl.when(z == k)
            def _():
                if targets:
                    wait(t_in.at[pl.ds(0, len(targets))], send.at[STATE_Z])

    def state_z_here():
        for k in range(nz):
            begin = k // half * half
            sources = [i for i in range(nz) if i <= begin + half - 2 and i != k]

            @pl.when((z == k) & is_owner)
            def _():
                if sources:
                    wait(t_in.at[pl.ds(0, len(sources))], recv.at[STATE_Z])

    leaving.append(state_z_left)
    arriving.append((STATE_Z, state_z_here))

    lax.fori_loop(1, early, forward, 0)

    arrived(RAW_Y)
    to_end, to_own = [None] * NY, [None] * NY
    after, after_own = jnp.zeros((NY, T), F32), jnp.zeros((NY, T), F32)
    for k in reversed(range(NY)):
        rest = tot[k] - raw[k, :NY]
        mine = jnp.full((NY, T), k, jnp.int32) < y
        to_end[k] = rest + after
        to_own[k] = jnp.where(mine, rest + after_own, 0.0)
        after = after + tot[k]
        after_own = after_own + jnp.where(mine, tot[k], 0.0)
    pieces = []
    for group in (to_end, to_own):
        logs = jnp.concatenate(group, axis=1)
        high = logs.astype(BF16).astype(F32)
        mid = (logs - high).astype(BF16).astype(F32)
        pieces += [high, mid, logs - high - mid]
    reach = lax.broadcasted_iota(jnp.int32, (NY, NY * T), 1) < y * T
    pieces += [jnp.ones((NY, NY * T), F32), jnp.where(reach, 1.0, 0.0)]
    hot = jnp.concatenate(
        [one_hot(jnp.broadcast_to(raw[k, pl.ds(NY, 1), :], (T, T)).T) for k in range(NY)], axis=0
    )
    table = dot(jnp.concatenate(pieces, axis=0).astype(BF16), hot)
    table = [table[i * NY:(i + 1) * NY] for i in range(8)]
    row_tab = jnp.where(table[6] > 0.5, table[0] + table[1] + table[2], FAR)
    own_tab = jnp.where(table[7] > 0.5, table[3] + table[4] + table[5], FAR)
    tab_z[z] = row_tab
    for to in z_peers():
        @pl.when(to > z)
        def _():
            put(tab_z.at[z], tab_z.at[z], TAB_Z, z_dev(to), RINGS[TAB_Z] + z)

    def tab_z_left():
        for k in range(nz):
            @pl.when(z == k)
            def _():
                if k < nz - 1:
                    wait(tab_z.at[pl.ds(0, nz - 1 - k)], send.at[TAB_Z])

    leaving.append(tab_z_left)

    def wide(a):
        return jnp.concatenate([a] * (vr // T), axis=1)

    lax.fori_loop(early, nz, forward, 0)
    slabs = fbuf.at[pl.ds(0, nx - 1)]
    expect(FEAT_X, slabs, slabs)

    arrived(TOT_Z)
    arrived(STATE_Z)

    @pl.when(is_owner)
    def _():
        t_in[z] = t_out[slot]

    for begin in (0, half):
        @pl.when(is_owner & (base == begin))
        def _():
            carry = jnp.zeros((share, T), F32)
            for k in range(begin + half):
                if k >= begin:
                    r_out[k] = carry
                if k < begin + half - 1:
                    carry = carry * jnp.exp(tot_z[k, pl.ds(y, 1), :]) + t_in[k]
            for k in range(max(begin, 2), begin + half):
                @pl.when(z != k)
                def _():
                    put(r_out.at[k], r_in.at[slot], BACK_Z, z_dev(k), RINGS[BACK_Z] + slot)

    @pl.when(is_owner & (z > 1))
    def _():
        r_in[slot] = r_out[z]

    def back_z_left():
        for k in range(nz):
            begin = k // half * half
            targets = [i for i in range(max(begin, 2), begin + half) if i != k]

            @pl.when((z == k) & is_owner)
            def _():
                if targets:
                    wait(r_out.at[pl.ds(0, len(targets))], send.at[BACK_Z])

        @pl.when(z == 0)
        def _():
            wait(t_out, send.at[BACK_Z])

    leaving.append(back_z_left)

    @pl.when(z == 1)
    def _():
        lax.fori_loop(0, owners, enter, 0)

    arrived(FEAT_X)
    for j in range(1, nx):
        slab = fbuf.at[core * nx + lax.rem(x + j, nx)]
        put(slab, slab, FEAT_C, h_dev(x * 2 + 1 - core))
    expect(FEAT_C, fbuf.at[pl.ds(0, nx)], fbuf.at[pl.ds(0, nx)])

    for copy in loads[5:]:
        copy.wait()
    chunk = 256

    def feature_half(side):
        columns = [fbuf[side * nx + j].reshape(vr, block_cols) for j in range(nx)]
        size = nx * block_cols
        return jnp.concatenate(columns, axis=1), pl.ds(pl.multiple_of(side * size, size), size)

    near_side, near_rows = feature_half(core)
    for m in range(2):
        for start in range(0, inner, chunk):
            cols = pl.ds(start, chunk)
            kv_sum[m, :, cols] = dot(near_side, w[m + 1, near_rows, cols])
    placed = dot(pick, near_side).astype(BF16)
    for start in range(0, inner, chunk):
        cols = pl.ds(start, chunk)
        query_sum[:, cols] = dot(placed, w[0, near_rows, cols])

    @pl.when(z > 1)
    def _():
        lax.fori_loop(0, owners, enter, 0)

    expect(BACK_Y, e_out.at[pl.ds(0, NY - 1)], e_in.at[pl.ds(0, NY - 1)])

    weight[...] = jnp.full((NY, vr), FAR, F32)
    for k in range(nz - 1):
        @pl.when(k < z)
        def _():
            wait(tab_z.at[k], recv.at[RINGS[TAB_Z] + k])
            weight[...] = jnp.maximum(weight[...] + wide(tot_z[k]), tab_z[k])

    weight[...] = jnp.exp(jnp.maximum(weight[...] + wide(pre[y]), own_tab))
    for h in range(NY):
        factor[h, :, :vr] = wide(grown[h]) * weight[pl.ds(h, 1), :]

    arrived(FEAT_C)
    far_side, far_rows = feature_half(1 - core)
    mask = jnp.concatenate([is_vis] * (chunk // T), axis=1)
    for m in range(2):
        for start in range(0, inner, chunk):
            cols = pl.ds(start, chunk)
            visual = (kv_sum[m, :, cols] + dot(far_side, w[m + 1, far_rows, cols])).astype(BF16)
            kv_all[m, :vr, cols] = visual
            own = jnp.where(mask, dot(pick, visual), text[m + 1, :, cols].astype(F32))
            kv_all[m, vr:, cols] = own.astype(BF16)
    placed = dot(pick, far_side).astype(BF16)
    for start in range(0, inner, chunk):
        cols = pl.ds(start, chunk)
        query = (query_sum[:, cols] + dot(placed, w[0, far_rows, cols])).astype(BF16).astype(F32)
        query_all[:, cols] = jnp.where(mask, query, text[0, :, cols].astype(F32)).astype(BF16)

    def head_within(h):
        at = lanes(h)
        query = query_all[:, at]
        weights = dot(query, kv_all[0, :, at], ((1,), (1,))) * factor[h]
        mixed[:, at] = dot(weights.astype(BF16), kv_all[1, :, at])

    for h in range(NY):
        head_within(h)

    arrived(BACK_Y)
    squares = jnp.zeros((T, T), F32)
    for h in range(NY):
        at = lanes(h)
        result = mixed[:, at] + grown[h] * dot(query_all[:, at], e_in[h])
        mixed[:, at] = result
        squares = squares + result * result

    norm[hd] = jnp.broadcast_to(jnp.sum(squares.T, axis=0, keepdims=True), (8, T))
    for k in range(1, nh):
        put(norm.at[hd], norm.at[hd], NORM, h_dev(lax.rem(hd + k, nh)))
    expect(NORM, norm.at[pl.ds(0, nh - 1)], norm.at[pl.ds(0, nh - 1)])
    arrived(NORM)
    square_sum = norm[0]
    for k in range(1, nh):
        square_sum = square_sum + norm[k]
    inverse = lax.rsqrt(square_sum * (1.0 / heads_total) + 1e-05)
    scale = jnp.broadcast_to(inverse[:1], (T, T)).T
    for h in range(NY):
        at = lanes(h)
        out[:, at] = (mixed[:, at] * scale * gain[:, at]).astype(BF16)

    finish()


def hbm(a):
    return pltpu.with_memory_space_constraint(a, pltpu.HBM)


def local(nz, nh, text_qkv, vis_feats, w_visual, vis_src, log_decay, norm_gain):
    row_count, _, inner = text_qkv.shape
    width = vis_feats.shape[1]
    vr = vis_feats.shape[0] * NY * nz
    _, owners, _ = halves(nz)
    share = T // owners
    vmem = pl.BlockSpec(memory_space=pltpu.VMEM)
    anywhere = pl.BlockSpec(memory_space=pltpu.HBM)
    scratch = [
        pltpu.VMEM((3, row_count, inner), BF16),
        pltpu.VMEM(vis_feats.shape, BF16),
        pltpu.VMEM((3, width, inner), BF16),
        pltpu.VMEM((1, row_count), jnp.int32),
        pltpu.VMEM(log_decay.shape, F32),
        pltpu.VMEM((1, inner), F32),
        pltpu.VMEM((NY, 4 * (nh // 2), width // nh), BF16),
        pltpu.VMEM((nh, nz, 4 * NY, width // nh), BF16),
        pltpu.VMEM((2, vr, inner), F32),
        pltpu.VMEM((row_count, inner), F32),
        pltpu.VMEM((2, vr + row_count, inner), BF16),
        pltpu.VMEM((row_count, inner), BF16),
        pltpu.VMEM((NY, T, T), BF16),
        pltpu.VMEM((NY, T, T), BF16),
        pltpu.VMEM((NY, T, T), BF16),
        pltpu.VMEM((NY, T, T), BF16),
        pltpu.VMEM((NY, T, T), F32),
        pltpu.VMEM((owners, share, T), F32),
        pltpu.VMEM((nz, share, T), F32),
        pltpu.VMEM((nz, share, T), F32),
        pltpu.VMEM((owners, share, T), F32),
        pltpu.VMEM((NY, 2 * NY, T), F32),
        pltpu.VMEM((NY, NY, T), F32),
        pltpu.VMEM((nz, NY, T), F32),
        pltpu.VMEM((NY, NY, T), F32),
        pltpu.VMEM((nz, NY, vr), F32),
        pltpu.VMEM((NY, vr), F32),
        pltpu.VMEM((NY, T, vr + T), F32),
        pltpu.VMEM((NY, T, T), F32),
        pltpu.VMEM((row_count, inner), F32),
        pltpu.VMEM((nh, 8, T), F32),
        pltpu.SemaphoreType.DMA((13,)),
        pltpu.SemaphoreType.DMA((RECEIVES,)),
        pltpu.SemaphoreType.DMA((8,)),
    ]
    return pl.pallas_call(
        functools.partial(kernel, nz, nh, inner * nh),
        out_shape=jax.ShapeDtypeStruct((row_count, inner), BF16),
        in_specs=[anywhere] * 6,
        out_specs=vmem,
        scratch_shapes=scratch,
        compiler_params=pltpu.CompilerParams(
            collective_id=0, has_side_effects=True, vmem_limit_bytes=48 * 1024 * 1024
        ),
        name="lightning",
    )(
        hbm(text_qkv.transpose(1, 0, 2)),
        hbm(vis_feats),
        hbm(w_visual.transpose(1, 0, 2)),
        hbm(vis_src.reshape(1, row_count)),
        hbm(log_decay),
        hbm(norm_gain.reshape(1, inner)),
    )


def solution(mesh):
    placed = (
        P("ctx", None, "head"),
        P("ctx", None),
        P(None, None, "head"),
        P("ctx"),
        P("head", "ctx"),
        P("head"),
    )
    nz, nh = mesh.shape["ctx"] // NY, mesh.shape["head"]
    return jax.shard_map(
        functools.partial(local, nz, nh), mesh=mesh, in_specs=placed, out_specs=P("ctx", "head"), check_vma=False
    )
```

```python
import functools

import jax
import jax.numpy as jnp
from jax import lax
from jax.experimental import pallas as pl
from jax.experimental.pallas import tpu as pltpu
from jax.sharding import PartitionSpec as P

MESH = pl.DeviceIdType.MESH
F32, BF16 = jnp.float32, jnp.bfloat16
NY = 8
FAR = -1e30
T = 128
TOT_Y, RAW_Y, FEAT_Y, TOT_Z, FEAT_X, FEAT_C, STATE_Z, BACK_Y, NORM, FEAT_Z, TAB_Z, BACK_Z, STATE_Y = range(13)
RINGS = {FEAT_X: 72, FEAT_Z: 16, TAB_Z: 32, BACK_Z: 48, STATE_Y: 64}
RECEIVES = 80


def halves(nz):
    half = nz // 2
    return (half, 4, 1) if half >= 6 else (half, half, 0)


def dot(a, b, dims=((1,), (0,))):
    return lax.dot_general(a, b, (dims, ((), ())), preferred_element_type=F32)


def lanes(h):
    start = h * T if isinstance(h, int) else pl.multiple_of(h * T, T)
    return pl.ds(start, T)


def kernel(
    nz, nh, heads_total,
    text_in, feats_in, w_in, vis_src_in, log_decay_in, gain_in, out,
    text, feats, w, vis_src, log_decay, gain, ybuf, fbuf, kv_sum, query_sum, kv_all, query_all, s_out, s_in, e_out, e_in, pstate,
    t_out, t_in, r_out, r_in, raw, tot, tot_z, pre, tab_z, weight, factor, grown, mixed, norm,
    send, recv, load,
):
    nx = nh // 2
    vr = kv_sum.shape[1]
    yrows = 4 * NY
    half, owners, first = halves(nz)
    share = T // owners
    block_cols = fbuf.shape[3]
    inner = w.shape[2]
    me, hd = lax.axis_index("ctx"), lax.axis_index("head")
    z, y = me // NY, me % NY
    x, core = hd // 2, hd % 2
    base = z // half * half
    slot = z - base - first
    is_owner = (slot >= 0) & (slot < owners)
    block = core * nx + x

    def y_dev(to):
        return {"ctx": z * NY + to, "head": hd}

    def z_dev(to):
        return {"ctx": to * NY + y, "head": hd}

    def h_dev(to):
        return {"ctx": me, "head": to}

    leaving, arriving = [], []

    def put(src, dst, phase, device, receive=None):
        pltpu.make_async_remote_copy(
            src_ref=src, dst_ref=dst, send_sem=send.at[phase], recv_sem=recv.at[phase if receive is None else receive],
            device_id=device, device_id_type=MESH,
        ).start()

    def wait(ref, sem):
        pltpu.make_async_copy(ref, ref, sem).wait()

    def expect(phase, ref_out, ref_in):
        leaving.append(lambda: wait(ref_out, send.at[phase]))
        arriving.append((phase, lambda: wait(ref_in, recv.at[phase])))

    def arrived(phase):
        (entry,) = [e for e in arriving if e[0] == phase]
        arriving.remove(entry)
        entry[1]()

    def finish():
        for waiting in leaving + [e for _, e in arriving]:
            waiting()

    def y_peers():
        return [lax.rem(y + k, NY) for k in (4, 3, 5, 2, 6, 1, 7)]

    def z_peers():
        return [lax.rem(z + k, nz) for k in sorted(range(1, nz), key=lambda k: -min(k, nz - k))]

    def near(k, here, count):
        return lax.rem(here + (k % 2 * 2 - 1) * ((k + 1) // 2) + count, count)

    barrier = pltpu.get_barrier_semaphore()
    for to in z_peers():
        pl.semaphore_signal(barrier, inc=1, device_id=z_dev(to), device_id_type=MESH)
    for to in y_peers():
        pl.semaphore_signal(barrier, inc=1, device_id=y_dev(to), device_id_type=MESH)
    for k in range(1, nh):
        pl.semaphore_signal(barrier, inc=1, device_id=h_dev(lax.rem(hd + k, nh)), device_id_type=MESH)

    pairs = [(feats_in, feats), (log_decay_in, log_decay), (vis_src_in, vis_src), (text_in.at[2], text.at[2]),
             (text_in.at[1], text.at[1]), (text_in.at[0], text.at[0]), (gain_in, gain), (w_in, w)]
    loads = [pltpu.make_async_copy(src, dst, load.at[i]) for i, (src, dst) in enumerate(pairs)]
    for copy in loads:
        copy.start()

    loads[0].wait()
    quarters = [
        feats[:, pl.ds(pl.multiple_of((core * nx + c) * block_cols, T), block_cols)].astype(F32) for c in range(nx)
    ]
    ybuf[y] = jnp.concatenate(quarters, axis=0).astype(BF16)

    loads[1].wait()
    lane = lax.broadcasted_iota(jnp.int32, (NY, T), 1)
    running = log_decay[...]
    step = 1
    while step < T:
        running = running + jnp.where(lane >= step, pltpu.roll(running, step, 1), 0.0)
        step *= 2

    def last_of(a):
        last = jnp.sum(jnp.where(lane == T - 1, a, 0.0), axis=1, keepdims=True)
        return jnp.broadcast_to(last, (NY, T))

    tot[y] = last_of(running)

    loads[2].wait()
    source_row = jnp.broadcast_to(vis_src[...], (T, T)).astype(F32)
    raw[y] = jnp.concatenate([running, source_row[:NY]], axis=0)
    source = source_row.T
    is_vis = source >= 0.0
    loads[3].wait()
    loads[4].wait()

    def head_state(h):
        row = jnp.broadcast_to(raw[y, pl.ds(h, 1), :], (T, T))
        last = jnp.broadcast_to(tot[y, pl.ds(h, 1), :], (T, T))
        tail = jnp.where(is_vis, 0.0, jnp.exp(last - row.T))
        value = text[2, :, lanes(h)].astype(F32) * tail
        high = value.astype(BF16)
        low = (value - high.astype(F32)).astype(BF16)
        both = dot(text[1, :, lanes(h)], jnp.concatenate([high, low], axis=1), ((0,), (0,)))
        s_out[h] = (both[:, :T] + both[:, T:]).astype(BF16)

    for h in range(NY):
        head_state(h)

    pl.semaphore_wait(barrier, NY - 1 + nz - 1 + nh - 1)
    for to in y_peers():
        put(ybuf.at[y], ybuf.at[y], FEAT_Y, y_dev(to))
    expect(FEAT_Y, ybuf.at[pl.ds(0, NY - 1)], ybuf.at[pl.ds(0, NY - 1)])
    for to in y_peers():
        put(tot.at[y], tot.at[y], TOT_Y, y_dev(to))
    expect(TOT_Y, tot.at[pl.ds(0, NY - 1)], tot.at[pl.ds(0, NY - 1)])
    for p in range(owners):
        at = pl.ds(p * share, share)
        for to in y_peers():
            put(s_out.at[to, at], s_in.at[y, at], STATE_Y, y_dev(to), RINGS[STATE_Y] + p)
    leaving.append(lambda: wait(s_out.at[pl.ds(0, NY - 1)], send.at[STATE_Y]))
    for to in y_peers():
        put(raw.at[y], raw.at[y], RAW_Y, y_dev(to))
    expect(RAW_Y, raw.at[pl.ds(0, NY - 1)], raw.at[pl.ds(0, NY - 1)])
    s_in[y] = s_out[y]

    row_id = lax.broadcasted_iota(jnp.int32, (1, vr), 1).astype(F32)

    def one_hot(column):
        return jnp.concatenate(
            [jnp.where(column == row_id[:, j:j + T], 1.0, 0.0) for j in range(0, vr, T)], axis=1
        ).astype(BF16)

    pick = one_hot(source)

    arrived(FEAT_Y)
    rows = lax.broadcasted_iota(jnp.int32, (yrows, 4 * nx * NY), 0)
    folded = lax.broadcasted_iota(jnp.int32, (yrows, 4 * nx * NY), 1)
    wanted = lax.shift_right_logical(rows, 2) * (4 * nx) + x * 4 + (rows & 3)
    unfold = jnp.where(wanted == folded, 1.0, 0.0).astype(BF16)
    fbuf[block, z] = dot(unfold, ybuf[...].reshape(4 * nx * NY, block_cols)).astype(BF16)
    for to in z_peers():
        put(fbuf.at[block, z], fbuf.at[block, z], FEAT_Z, z_dev(to), RINGS[FEAT_Z] + z)
    leaving.append(lambda: wait(fbuf.at[0, pl.ds(0, nz - 1)], send.at[FEAT_Z]))

    arrived(TOT_Y)
    before = jnp.zeros((NY, T), F32)
    for k in range(NY):
        pre[k] = before
        before = before + tot[k]
    tot_z[z] = before
    for to in z_peers():
        put(tot_z.at[z], tot_z.at[z], TOT_Z, z_dev(to))
    expect(TOT_Z, tot_z.at[pl.ds(0, nz - 1)], tot_z.at[pl.ds(0, nz - 1)])

    def forward(k, _):
        piece = fbuf.at[block, near(k, z, nz)]

        @pl.when(k > 0)
        def _():
            wait(piece, recv.at[RINGS[FEAT_Z] + near(k, z, nz)])

        for j in range(1, nx):
            put(piece, piece, FEAT_X, h_dev(lax.rem(x + j, nx) * 2 + core), RINGS[FEAT_X] + x)
        put(piece, piece, FEAT_C, h_dev(x * 2 + 1 - core))
        return 0

    lax.fori_loop(0, 1, forward, 0)

    causal = lax.broadcasted_iota(jnp.int32, (T, T), 0) >= lax.broadcasted_iota(jnp.int32, (T, T), 1)

    def head_decay(h):
        row = jnp.broadcast_to(raw[y, pl.ds(h, 1), :], (T, T))
        col = row.T
        grown[h] = jnp.exp(col)
        factor[h, :, vr:] = jnp.where(causal, jnp.exp(jnp.where(causal, col - row, 0.0)), 0.0)

    for h in range(NY):
        head_decay(h)

    early = nz // 2 + 1
    for p in range(owners):
        at = pl.ds(p * share, share)
        wait(s_in.at[pl.ds(0, NY - 1), at], recv.at[RINGS[STATE_Y] + p])
        state = jnp.zeros((share, T), F32)
        for k in range(NY):
            pstate[k, at] = state
            state = state * jnp.exp(tot[k, pl.ds(y, 1), :]) + s_in[k, at].astype(F32)
        t_out[p] = state

        @pl.when(z == 0)
        def _():
            put(t_out.at[p], r_in.at[p], BACK_Z, z_dev(1), RINGS[BACK_Z] + p)

        for begin, last in ((0, half - 2), (half, nz - 2)):
            owner = begin + first + p

            @pl.when((z != owner) & (z <= last))
            def _():
                put(t_out.at[p], t_in.at[z], STATE_Z, z_dev(owner))

    def enter(owner, _):
        @pl.when((z == 1) | ((z > 1) & (owner != slot)))
        def _():
            wait(r_in.at[owner], recv.at[RINGS[BACK_Z] + owner])

        at = pl.ds(pl.multiple_of(owner * share, share), share)
        entering = r_in[owner]
        for to in y_peers():
            e_out[to, at] = (pstate[to, at] + entering * jnp.exp(pre[to, pl.ds(y, 1), :])).astype(BF16)
            put(e_out.at[to, at], e_in.at[y, at], BACK_Y, y_dev(to))
        e_in[y, at] = (pstate[y, at] + entering * jnp.exp(pre[y, pl.ds(y, 1), :])).astype(BF16)
        return 0

    @pl.when(z == 0)
    def _():
        r_in[...] = jnp.zeros_like(r_in)
        lax.fori_loop(0, owners, enter, 0)

    def state_z_left():
        for k in range(nz):
            targets = [
                begin + first + p for begin, last in ((0, half - 2), (half, nz - 2)) if k <= last for p in range(owners)
                if begin + first + p != k
            ]

            @pl.when(z == k)
            def _():
                if targets:
                    wait(t_in.at[pl.ds(0, len(targets))], send.at[STATE_Z])

    def state_z_here():
        for k in range(nz):
            begin = k // half * half
            sources = [i for i in range(nz) if i <= begin + half - 2 and i != k]

            @pl.when((z == k) & is_owner)
            def _():
                if sources:
                    wait(t_in.at[pl.ds(0, len(sources))], recv.at[STATE_Z])

    leaving.append(state_z_left)
    arriving.append((STATE_Z, state_z_here))

    lax.fori_loop(1, early, forward, 0)

    arrived(RAW_Y)
    to_end, to_own = [None] * NY, [None] * NY
    after, after_own = jnp.zeros((NY, T), F32), jnp.zeros((NY, T), F32)
    for k in reversed(range(NY)):
        rest = tot[k] - raw[k, :NY]
        mine = jnp.full((NY, T), k, jnp.int32) < y
        to_end[k] = rest + after
        to_own[k] = jnp.where(mine, rest + after_own, 0.0)
        after = after + tot[k]
        after_own = after_own + jnp.where(mine, tot[k], 0.0)
    pieces = []
    for group in (to_end, to_own):
        logs = jnp.concatenate(group, axis=1)
        high = logs.astype(BF16).astype(F32)
        mid = (logs - high).astype(BF16).astype(F32)
        pieces += [high, mid, logs - high - mid]
    reach = lax.broadcasted_iota(jnp.int32, (NY, NY * T), 1) < y * T
    pieces += [jnp.ones((NY, NY * T), F32), jnp.where(reach, 1.0, 0.0)]
    hot = jnp.concatenate(
        [one_hot(jnp.broadcast_to(raw[k, pl.ds(NY, 1), :], (T, T)).T) for k in range(NY)], axis=0
    )
    table = dot(jnp.concatenate(pieces, axis=0).astype(BF16), hot)
    table = [table[i * NY:(i + 1) * NY] for i in range(8)]
    row_tab = jnp.where(table[6] > 0.5, table[0] + table[1] + table[2], FAR)
    own_tab = jnp.where(table[7] > 0.5, table[3] + table[4] + table[5], FAR)
    tab_z[z] = row_tab
    def tab_z_left():
        for k in range(nz):
            @pl.when(z == k)
            def _():
                if k < nz - 1:
                    wait(tab_z.at[pl.ds(0, nz - 1 - k)], send.at[TAB_Z])

    leaving.append(tab_z_left)

    def wide(a):
        return jnp.concatenate([a] * (vr // T), axis=1)

    lax.fori_loop(early, nz, forward, 0)
    leaving.append(lambda: wait(fbuf.at[pl.ds(0, nx - 1)], send.at[FEAT_X]))

    arrived(TOT_Z)
    arrived(STATE_Z)

    @pl.when(is_owner)
    def _():
        t_in[z] = t_out[slot]

    for begin in (0, half):
        @pl.when(is_owner & (base == begin))
        def _():
            carry = jnp.zeros((share, T), F32)
            for k in range(begin + half):
                if k >= begin:
                    r_out[k] = carry
                if k < begin + half - 1:
                    carry = carry * jnp.exp(tot_z[k, pl.ds(y, 1), :]) + t_in[k]
            for k in range(max(begin, 2), begin + half):
                @pl.when(z != k)
                def _():
                    put(r_out.at[k], r_in.at[slot], BACK_Z, z_dev(k), RINGS[BACK_Z] + slot)

    @pl.when(is_owner & (z > 1))
    def _():
        r_in[slot] = r_out[z]

    def back_z_left():
        for k in range(nz):
            begin = k // half * half
            targets = [i for i in range(max(begin, 2), begin + half) if i != k]

            @pl.when((z == k) & is_owner)
            def _():
                if targets:
                    wait(r_out.at[pl.ds(0, len(targets))], send.at[BACK_Z])

        @pl.when(z == 0)
        def _():
            wait(t_out, send.at[BACK_Z])

    leaving.append(back_z_left)

    for to in z_peers():
        @pl.when(to > z)
        def _():
            put(tab_z.at[z], tab_z.at[z], TAB_Z, z_dev(to), RINGS[TAB_Z] + z)

    @pl.when(z == 1)
    def _():
        lax.fori_loop(0, owners, enter, 0)

    for j in sorted(range(1, nx), key=lambda j: min(j, nx - j)):
        slab = fbuf.at[core * nx + lax.rem(x + j, nx)]
        wait(slab, recv.at[RINGS[FEAT_X] + lax.rem(x + j, nx)])
        put(slab, slab, FEAT_C, h_dev(x * 2 + 1 - core))
    expect(FEAT_C, fbuf.at[pl.ds(0, nx)], fbuf.at[pl.ds(0, nx)])

    for copy in loads[5:]:
        copy.wait()
    chunk = 256

    def feature_half(side):
        columns = [fbuf[side * nx + j].reshape(vr, block_cols) for j in range(nx)]
        size = nx * block_cols
        return jnp.concatenate(columns, axis=1), pl.ds(pl.multiple_of(side * size, size), size)

    near_side, near_rows = feature_half(core)
    for m in range(2):
        for start in range(0, inner, chunk):
            cols = pl.ds(start, chunk)
            kv_sum[m, :, cols] = dot(near_side, w[m + 1, near_rows, cols])
    placed = dot(pick, near_side).astype(BF16)
    for start in range(0, inner, chunk):
        cols = pl.ds(start, chunk)
        query_sum[:, cols] = dot(placed, w[0, near_rows, cols])

    @pl.when(z > 1)
    def _():
        lax.fori_loop(0, owners, enter, 0)

    expect(BACK_Y, e_out.at[pl.ds(0, NY - 1)], e_in.at[pl.ds(0, NY - 1)])

    weight[...] = jnp.full((NY, vr), FAR, F32)
    for k in range(nz - 1):
        @pl.when(k < z)
        def _():
            wait(tab_z.at[k], recv.at[RINGS[TAB_Z] + k])
            weight[...] = jnp.maximum(weight[...] + wide(tot_z[k]), tab_z[k])

    weight[...] = jnp.exp(jnp.maximum(weight[...] + wide(pre[y]), own_tab))
    for h in range(NY):
        factor[h, :, :vr] = wide(grown[h]) * weight[pl.ds(h, 1), :]

    arrived(FEAT_C)
    far_side, far_rows = feature_half(1 - core)
    mask = jnp.concatenate([is_vis] * (chunk // T), axis=1)
    for m in range(2):
        for start in range(0, inner, chunk):
            cols = pl.ds(start, chunk)
            visual = (kv_sum[m, :, cols] + dot(far_side, w[m + 1, far_rows, cols])).astype(BF16)
            kv_all[m, :vr, cols] = visual
            own = jnp.where(mask, dot(pick, visual), text[m + 1, :, cols].astype(F32))
            kv_all[m, vr:, cols] = own.astype(BF16)
    placed = dot(pick, far_side).astype(BF16)
    for start in range(0, inner, chunk):
        cols = pl.ds(start, chunk)
        query = (query_sum[:, cols] + dot(placed, w[0, far_rows, cols])).astype(BF16).astype(F32)
        query_all[:, cols] = jnp.where(mask, query, text[0, :, cols].astype(F32)).astype(BF16)

    def head_within(h):
        at = lanes(h)
        query = query_all[:, at]
        weights = dot(query, kv_all[0, :, at], ((1,), (1,))) * factor[h]
        mixed[:, at] = dot(weights.astype(BF16), kv_all[1, :, at])

    for h in range(NY):
        head_within(h)

    arrived(BACK_Y)
    squares = jnp.zeros((T, T), F32)
    for h in range(NY):
        at = lanes(h)
        result = mixed[:, at] + grown[h] * dot(query_all[:, at], e_in[h])
        mixed[:, at] = result
        squares = squares + result * result

    norm[hd] = jnp.broadcast_to(jnp.sum(squares.T, axis=0, keepdims=True), (8, T))
    for k in range(1, nh):
        put(norm.at[hd], norm.at[hd], NORM, h_dev(lax.rem(hd + k, nh)))
    expect(NORM, norm.at[pl.ds(0, nh - 1)], norm.at[pl.ds(0, nh - 1)])
    finish()
    square_sum = norm[0]
    for k in range(1, nh):
        square_sum = square_sum + norm[k]
    inverse = lax.rsqrt(square_sum * (1.0 / heads_total) + 1e-05)
    scale = jnp.broadcast_to(inverse[:1], (T, T)).T
    for h in range(NY):
        at = lanes(h)
        out[:, at] = (mixed[:, at] * scale * gain[:, at]).astype(BF16)


def hbm(a):
    return pltpu.with_memory_space_constraint(a, pltpu.HBM)


def local(nz, nh, text_qkv, vis_feats, w_visual, vis_src, log_decay, norm_gain):
    row_count, _, inner = text_qkv.shape
    width = vis_feats.shape[1]
    vr = vis_feats.shape[0] * NY * nz
    _, owners, _ = halves(nz)
    share = T // owners
    vmem = pl.BlockSpec(memory_space=pltpu.VMEM)
    anywhere = pl.BlockSpec(memory_space=pltpu.HBM)
    scratch = [
        pltpu.VMEM((3, row_count, inner), BF16),
        pltpu.VMEM(vis_feats.shape, BF16),
        pltpu.VMEM((3, width, inner), BF16),
        pltpu.VMEM((1, row_count), jnp.int32),
        pltpu.VMEM(log_decay.shape, F32),
        pltpu.VMEM((1, inner), F32),
        pltpu.VMEM((NY, 4 * (nh // 2), width // nh), BF16),
        pltpu.VMEM((nh, nz, 4 * NY, width // nh), BF16),
        pltpu.VMEM((2, vr, inner), F32),
        pltpu.VMEM((row_count, inner), F32),
        pltpu.VMEM((2, vr + row_count, inner), BF16),
        pltpu.VMEM((row_count, inner), BF16),
        pltpu.VMEM((NY, T, T), BF16),
        pltpu.VMEM((NY, T, T), BF16),
        pltpu.VMEM((NY, T, T), BF16),
        pltpu.VMEM((NY, T, T), BF16),
        pltpu.VMEM((NY, T, T), F32),
        pltpu.VMEM((owners, share, T), F32),
        pltpu.VMEM((nz, share, T), F32),
        pltpu.VMEM((nz, share, T), F32),
        pltpu.VMEM((owners, share, T), F32),
        pltpu.VMEM((NY, 2 * NY, T), F32),
        pltpu.VMEM((NY, NY, T), F32),
        pltpu.VMEM((nz, NY, T), F32),
        pltpu.VMEM((NY, NY, T), F32),
        pltpu.VMEM((nz, NY, vr), F32),
        pltpu.VMEM((NY, vr), F32),
        pltpu.VMEM((NY, T, vr + T), F32),
        pltpu.VMEM((NY, T, T), F32),
        pltpu.VMEM((row_count, inner), F32),
        pltpu.VMEM((nh, 8, T), F32),
        pltpu.SemaphoreType.DMA((13,)),
        pltpu.SemaphoreType.DMA((RECEIVES,)),
        pltpu.SemaphoreType.DMA((8,)),
    ]
    return pl.pallas_call(
        functools.partial(kernel, nz, nh, inner * nh),
        out_shape=jax.ShapeDtypeStruct((row_count, inner), BF16),
        in_specs=[anywhere] * 6,
        out_specs=vmem,
        scratch_shapes=scratch,
        compiler_params=pltpu.CompilerParams(
            collective_id=0, has_side_effects=True, vmem_limit_bytes=48 * 1024 * 1024
        ),
        name="lightning",
    )(
        hbm(text_qkv.transpose(1, 0, 2)),
        hbm(vis_feats),
        hbm(w_visual.transpose(1, 0, 2)),
        hbm(vis_src.reshape(1, row_count)),
        hbm(log_decay),
        hbm(norm_gain.reshape(1, inner)),
    )


def solution(mesh):
    placed = (
        P("ctx", None, "head"),
        P("ctx", None),
        P(None, None, "head"),
        P("ctx"),
        P("head", "ctx"),
        P("head"),
    )
    nz, nh = mesh.shape["ctx"] // NY, mesh.shape["head"]
    return jax.shard_map(
        functools.partial(local, nz, nh), mesh=mesh, in_specs=placed, out_specs=P("ctx", "head"), check_vma=False
    )
```

```python
import functools

import jax
import jax.numpy as jnp
from jax import lax
from jax.experimental import pallas as pl
from jax.experimental.pallas import tpu as pltpu
from jax.sharding import PartitionSpec as P

MESH = pl.DeviceIdType.MESH
F32, BF16 = jnp.float32, jnp.bfloat16
NY = 8
FAR = -1e30
T = 128
TOT_Y, RAW_Y, FEAT_Y, TOT_Z, FEAT_X, FEAT_C, STATE_Z, BACK_Y, NORM, FEAT_Z, TAB_Z, BACK_Z, STATE_Y = range(13)
RINGS = {FEAT_X: 72, FEAT_Z: 16, TAB_Z: 32, BACK_Z: 48, STATE_Y: 64}
RECEIVES = 80


def halves(nz):
    half = nz // 2
    return (half, 4, 1) if half >= 6 else (half, half, 0)


def dot(a, b, dims=((1,), (0,))):
    return lax.dot_general(a, b, (dims, ((), ())), preferred_element_type=F32)


def lanes(h):
    start = h * T if isinstance(h, int) else pl.multiple_of(h * T, T)
    return pl.ds(start, T)


def kernel(
    nz, nh, heads_total,
    text_in, feats_in, w_in, vis_src_in, log_decay_in, gain_in, out,
    text, feats, w, vis_src, log_decay, gain, ybuf, fbuf, kv_sum, query_sum, query_all, s_out, s_in, e_out, e_in, pstate,
    t_out, t_in, r_out, r_in, raw, tot, tot_z, pre, tab_z, weight, factor, grown, mixed, norm,
    send, recv, load,
):
    nx = nh // 2
    vr = kv_sum.shape[1]
    yrows = 4 * NY
    half, owners, first = halves(nz)
    share = T // owners
    block_cols = fbuf.shape[3]
    inner = w.shape[2]
    me, hd = lax.axis_index("ctx"), lax.axis_index("head")
    z, y = me // NY, me % NY
    x, core = hd // 2, hd % 2
    base = z // half * half
    slot = z - base - first
    is_owner = (slot >= 0) & (slot < owners)
    block = core * nx + x

    def y_dev(to):
        return {"ctx": z * NY + to, "head": hd}

    def z_dev(to):
        return {"ctx": to * NY + y, "head": hd}

    def h_dev(to):
        return {"ctx": me, "head": to}

    leaving, arriving = [], []

    def put(src, dst, phase, device, receive=None):
        pltpu.make_async_remote_copy(
            src_ref=src, dst_ref=dst, send_sem=send.at[phase], recv_sem=recv.at[phase if receive is None else receive],
            device_id=device, device_id_type=MESH,
        ).start()

    def wait(ref, sem):
        pltpu.make_async_copy(ref, ref, sem).wait()

    def expect(phase, ref_out, ref_in):
        leaving.append(lambda: wait(ref_out, send.at[phase]))
        arriving.append((phase, lambda: wait(ref_in, recv.at[phase])))

    def arrived(phase):
        (entry,) = [e for e in arriving if e[0] == phase]
        arriving.remove(entry)
        entry[1]()

    def finish():
        for waiting in leaving + [e for _, e in arriving]:
            waiting()

    def y_peers():
        return [lax.rem(y + k, NY) for k in (4, 3, 5, 2, 6, 1, 7)]

    def z_peers():
        return [lax.rem(z + k, nz) for k in sorted(range(1, nz), key=lambda k: -min(k, nz - k))]

    def near(k, here, count):
        return lax.rem(here + (k % 2 * 2 - 1) * ((k + 1) // 2) + count, count)

    barrier = pltpu.get_barrier_semaphore()
    for to in z_peers():
        pl.semaphore_signal(barrier, inc=1, device_id=z_dev(to), device_id_type=MESH)
    for to in y_peers():
        pl.semaphore_signal(barrier, inc=1, device_id=y_dev(to), device_id_type=MESH)
    for k in range(1, nh):
        pl.semaphore_signal(barrier, inc=1, device_id=h_dev(lax.rem(hd + k, nh)), device_id_type=MESH)

    pairs = [(feats_in, feats), (log_decay_in, log_decay), (vis_src_in, vis_src), (text_in.at[2], text.at[2]),
             (text_in.at[1], text.at[1]), (text_in.at[0], text.at[0]), (gain_in, gain), (w_in, w)]
    loads = [pltpu.make_async_copy(src, dst, load.at[i]) for i, (src, dst) in enumerate(pairs)]
    for copy in loads:
        copy.start()

    loads[0].wait()
    quarters = [
        feats[:, pl.ds(pl.multiple_of((core * nx + c) * block_cols, T), block_cols)].astype(F32) for c in range(nx)
    ]
    ybuf[y] = jnp.concatenate(quarters, axis=0).astype(BF16)

    loads[1].wait()
    lane = lax.broadcasted_iota(jnp.int32, (NY, T), 1)
    running = log_decay[...]
    step = 1
    while step < T:
        running = running + jnp.where(lane >= step, pltpu.roll(running, step, 1), 0.0)
        step *= 2

    def last_of(a):
        last = jnp.sum(jnp.where(lane == T - 1, a, 0.0), axis=1, keepdims=True)
        return jnp.broadcast_to(last, (NY, T))

    tot[y] = last_of(running)

    loads[2].wait()
    source_row = jnp.broadcast_to(vis_src[...], (T, T)).astype(F32)
    raw[y] = jnp.concatenate([running, source_row[:NY]], axis=0)
    source = source_row.T
    is_vis = source >= 0.0
    loads[3].wait()
    loads[4].wait()

    def head_state(h):
        row = jnp.broadcast_to(raw[y, pl.ds(h, 1), :], (T, T))
        last = jnp.broadcast_to(tot[y, pl.ds(h, 1), :], (T, T))
        tail = jnp.where(is_vis, 0.0, jnp.exp(last - row.T))
        value = text[2, :, lanes(h)].astype(F32) * tail
        high = value.astype(BF16)
        low = (value - high.astype(F32)).astype(BF16)
        both = dot(text[1, :, lanes(h)], jnp.concatenate([high, low], axis=1), ((0,), (0,)))
        s_out[h] = (both[:, :T] + both[:, T:]).astype(BF16)

    for h in range(NY):
        head_state(h)

    pl.semaphore_wait(barrier, NY - 1 + nz - 1 + nh - 1)
    for to in y_peers():
        put(ybuf.at[y], ybuf.at[y], FEAT_Y, y_dev(to))
    expect(FEAT_Y, ybuf.at[pl.ds(0, NY - 1)], ybuf.at[pl.ds(0, NY - 1)])
    for to in y_peers():
        put(tot.at[y], tot.at[y], TOT_Y, y_dev(to))
    expect(TOT_Y, tot.at[pl.ds(0, NY - 1)], tot.at[pl.ds(0, NY - 1)])
    for p in range(owners):
        at = pl.ds(p * share, share)
        for to in y_peers():
            put(s_out.at[to, at], s_in.at[y, at], STATE_Y, y_dev(to), RINGS[STATE_Y] + p)
    leaving.append(lambda: wait(s_out.at[pl.ds(0, NY - 1)], send.at[STATE_Y]))
    for to in y_peers():
        put(raw.at[y], raw.at[y], RAW_Y, y_dev(to))
    expect(RAW_Y, raw.at[pl.ds(0, NY - 1)], raw.at[pl.ds(0, NY - 1)])
    s_in[y] = s_out[y]

    row_id = lax.broadcasted_iota(jnp.int32, (1, vr), 1).astype(F32)

    def one_hot(column):
        return jnp.concatenate(
            [jnp.where(column == row_id[:, j:j + T], 1.0, 0.0) for j in range(0, vr, T)], axis=1
        ).astype(BF16)

    pick = one_hot(source)

    arrived(FEAT_Y)
    rows = lax.broadcasted_iota(jnp.int32, (yrows, 4 * nx * NY), 0)
    folded = lax.broadcasted_iota(jnp.int32, (yrows, 4 * nx * NY), 1)
    wanted = lax.shift_right_logical(rows, 2) * (4 * nx) + x * 4 + (rows & 3)
    unfold = jnp.where(wanted == folded, 1.0, 0.0).astype(BF16)
    fbuf[block, z] = dot(unfold, ybuf[...].reshape(4 * nx * NY, block_cols)).astype(BF16)
    for to in z_peers():
        put(fbuf.at[block, z], fbuf.at[block, z], FEAT_Z, z_dev(to), RINGS[FEAT_Z] + z)
    leaving.append(lambda: wait(fbuf.at[0, pl.ds(0, nz - 1)], send.at[FEAT_Z]))

    arrived(TOT_Y)
    before = jnp.zeros((NY, T), F32)
    for k in range(NY):
        pre[k] = before
        before = before + tot[k]
    tot_z[z] = before
    for to in z_peers():
        put(tot_z.at[z], tot_z.at[z], TOT_Z, z_dev(to))
    expect(TOT_Z, tot_z.at[pl.ds(0, nz - 1)], tot_z.at[pl.ds(0, nz - 1)])

    def forward(k, _):
        piece = fbuf.at[block, near(k, z, nz)]

        @pl.when(k > 0)
        def _():
            wait(piece, recv.at[RINGS[FEAT_Z] + near(k, z, nz)])

        for j in range(1, nx):
            put(piece, piece, FEAT_X, h_dev(lax.rem(x + j, nx) * 2 + core), RINGS[FEAT_X] + x)
        put(piece, piece, FEAT_C, h_dev(x * 2 + 1 - core))
        return 0

    lax.fori_loop(0, 1, forward, 0)

    causal = lax.broadcasted_iota(jnp.int32, (T, T), 0) >= lax.broadcasted_iota(jnp.int32, (T, T), 1)

    def head_decay(h):
        row = jnp.broadcast_to(raw[y, pl.ds(h, 1), :], (T, T))
        col = row.T
        grown[h] = jnp.exp(col)
        factor[h, :, vr:] = jnp.where(causal, jnp.exp(jnp.where(causal, col - row, 0.0)), 0.0)

    for h in range(NY):
        head_decay(h)

    early = nz // 2 + 1
    for p in range(owners):
        at = pl.ds(p * share, share)
        wait(s_in.at[pl.ds(0, NY - 1), at], recv.at[RINGS[STATE_Y] + p])
        state = jnp.zeros((share, T), F32)
        for k in range(NY):
            pstate[k, at] = state
            state = state * jnp.exp(tot[k, pl.ds(y, 1), :]) + s_in[k, at].astype(F32)
        t_out[p] = state

        @pl.when(z == 0)
        def _():
            put(t_out.at[p], r_in.at[p], BACK_Z, z_dev(1), RINGS[BACK_Z] + p)

        for begin, last in ((0, half - 2), (half, nz - 2)):
            owner = begin + first + p

            @pl.when((z != owner) & (z <= last))
            def _():
                put(t_out.at[p], t_in.at[z], STATE_Z, z_dev(owner))

    def enter(owner, _):
        @pl.when((z == 1) | ((z > 1) & (owner != slot)))
        def _():
            wait(r_in.at[owner], recv.at[RINGS[BACK_Z] + owner])

        at = pl.ds(pl.multiple_of(owner * share, share), share)
        entering = r_in[owner]
        for to in y_peers():
            e_out[to, at] = (pstate[to, at] + entering * jnp.exp(pre[to, pl.ds(y, 1), :])).astype(BF16)
            put(e_out.at[to, at], e_in.at[y, at], BACK_Y, y_dev(to))
        e_in[y, at] = (pstate[y, at] + entering * jnp.exp(pre[y, pl.ds(y, 1), :])).astype(BF16)
        return 0

    @pl.when(z == 0)
    def _():
        r_in[...] = jnp.zeros_like(r_in)
        lax.fori_loop(0, owners, enter, 0)

    def state_z_left():
        for k in range(nz):
            targets = [
                begin + first + p for begin, last in ((0, half - 2), (half, nz - 2)) if k <= last for p in range(owners)
                if begin + first + p != k
            ]

            @pl.when(z == k)
            def _():
                if targets:
                    wait(t_in.at[pl.ds(0, len(targets))], send.at[STATE_Z])

    def state_z_here():
        for k in range(nz):
            begin = k // half * half
            sources = [i for i in range(nz) if i <= begin + half - 2 and i != k]

            @pl.when((z == k) & is_owner)
            def _():
                if sources:
                    wait(t_in.at[pl.ds(0, len(sources))], recv.at[STATE_Z])

    leaving.append(state_z_left)
    arriving.append((STATE_Z, state_z_here))

    lax.fori_loop(1, early, forward, 0)

    arrived(RAW_Y)
    to_end, to_own = [None] * NY, [None] * NY
    after, after_own = jnp.zeros((NY, T), F32), jnp.zeros((NY, T), F32)
    for k in reversed(range(NY)):
        rest = tot[k] - raw[k, :NY]
        mine = jnp.full((NY, T), k, jnp.int32) < y
        to_end[k] = rest + after
        to_own[k] = jnp.where(mine, rest + after_own, 0.0)
        after = after + tot[k]
        after_own = after_own + jnp.where(mine, tot[k], 0.0)
    pieces = []
    for group in (to_end, to_own):
        logs = jnp.concatenate(group, axis=1)
        high = logs.astype(BF16).astype(F32)
        mid = (logs - high).astype(BF16).astype(F32)
        pieces += [high, mid, logs - high - mid]
    reach = lax.broadcasted_iota(jnp.int32, (NY, NY * T), 1) < y * T
    pieces += [jnp.ones((NY, NY * T), F32), jnp.where(reach, 1.0, 0.0)]
    hot = jnp.concatenate(
        [one_hot(jnp.broadcast_to(raw[k, pl.ds(NY, 1), :], (T, T)).T) for k in range(NY)], axis=0
    )
    table = dot(jnp.concatenate(pieces, axis=0).astype(BF16), hot)
    table = [table[i * NY:(i + 1) * NY] for i in range(8)]
    row_tab = jnp.where(table[6] > 0.5, table[0] + table[1] + table[2], FAR)
    own_tab = jnp.where(table[7] > 0.5, table[3] + table[4] + table[5], FAR)
    tab_z[z] = row_tab
    def tab_z_left():
        for k in range(nz):
            @pl.when(z == k)
            def _():
                if k < nz - 1:
                    wait(tab_z.at[pl.ds(0, nz - 1 - k)], send.at[TAB_Z])

    leaving.append(tab_z_left)

    def wide(a):
        return jnp.concatenate([a] * (vr // T), axis=1)

    lax.fori_loop(early, nz, forward, 0)
    leaving.append(lambda: wait(fbuf.at[pl.ds(0, nx - 1)], send.at[FEAT_X]))

    arrived(TOT_Z)
    arrived(STATE_Z)

    @pl.when(is_owner)
    def _():
        t_in[z] = t_out[slot]

    for begin in (0, half):
        @pl.when(is_owner & (base == begin))
        def _():
            carry = jnp.zeros((share, T), F32)
            for k in range(begin + half):
                if k >= begin:
                    r_out[k] = carry
                if k < begin + half - 1:
                    carry = carry * jnp.exp(tot_z[k, pl.ds(y, 1), :]) + t_in[k]
            for k in range(max(begin, 2), begin + half):
                @pl.when(z != k)
                def _():
                    put(r_out.at[k], r_in.at[slot], BACK_Z, z_dev(k), RINGS[BACK_Z] + slot)

    @pl.when(is_owner & (z > 1))
    def _():
        r_in[slot] = r_out[z]

    def back_z_left():
        for k in range(nz):
            begin = k // half * half
            targets = [i for i in range(max(begin, 2), begin + half) if i != k]

            @pl.when((z == k) & is_owner)
            def _():
                if targets:
                    wait(r_out.at[pl.ds(0, len(targets))], send.at[BACK_Z])

        @pl.when(z == 0)
        def _():
            wait(t_out, send.at[BACK_Z])

    leaving.append(back_z_left)

    for to in z_peers():
        @pl.when(to > z)
        def _():
            put(tab_z.at[z], tab_z.at[z], TAB_Z, z_dev(to), RINGS[TAB_Z] + z)

    @pl.when(z == 1)
    def _():
        lax.fori_loop(0, owners, enter, 0)

    for j in sorted(range(1, nx), key=lambda j: min(j, nx - j)):
        slab = fbuf.at[core * nx + lax.rem(x + j, nx)]
        wait(slab, recv.at[RINGS[FEAT_X] + lax.rem(x + j, nx)])
        put(slab, slab, FEAT_C, h_dev(x * 2 + 1 - core))
    expect(FEAT_C, fbuf.at[pl.ds(0, nx)], fbuf.at[pl.ds(0, nx)])

    for copy in loads[5:]:
        copy.wait()
    chunk = 256

    def feature_half(side):
        columns = [fbuf[side * nx + j].reshape(vr, block_cols) for j in range(nx)]
        size = nx * block_cols
        return jnp.concatenate(columns, axis=1), pl.ds(pl.multiple_of(side * size, size), size)

    near_side, near_rows = feature_half(core)
    for m in range(2):
        for start in range(0, inner, chunk):
            cols = pl.ds(start, chunk)
            kv_sum[m, :, cols] = dot(near_side, w[m + 1, near_rows, cols])
    placed = dot(pick, near_side).astype(BF16)
    for start in range(0, inner, chunk):
        cols = pl.ds(start, chunk)
        query_sum[:, cols] = dot(placed, w[0, near_rows, cols])

    @pl.when(z > 1)
    def _():
        lax.fori_loop(0, owners, enter, 0)

    expect(BACK_Y, e_out.at[pl.ds(0, NY - 1)], e_in.at[pl.ds(0, NY - 1)])

    weight[...] = jnp.full((NY, vr), FAR, F32)
    for k in range(nz - 1):
        @pl.when(k < z)
        def _():
            wait(tab_z.at[k], recv.at[RINGS[TAB_Z] + k])
            weight[...] = jnp.maximum(weight[...] + wide(tot_z[k]), tab_z[k])

    weight[...] = jnp.exp(jnp.maximum(weight[...] + wide(pre[y]), own_tab))
    for h in range(NY):
        factor[h, :, :vr] = wide(grown[h]) * weight[pl.ds(h, 1), :]

    arrived(FEAT_C)
    far_side, far_rows = feature_half(1 - core)
    mask = jnp.concatenate([is_vis] * (chunk // T), axis=1)
    placed = dot(pick, far_side).astype(BF16)
    for start in range(0, inner, chunk):
        cols = pl.ds(start, chunk)
        keys_values = []
        for m in range(2):
            visual = (kv_sum[m, :, cols] + dot(far_side, w[m + 1, far_rows, cols])).astype(BF16)
            own = jnp.where(mask, dot(pick, visual), text[m + 1, :, cols].astype(F32)).astype(BF16)
            keys_values.append(jnp.concatenate([visual, own], axis=0))
        query = (query_sum[:, cols] + dot(placed, w[0, far_rows, cols])).astype(BF16).astype(F32)
        query = jnp.where(mask, query, text[0, :, cols].astype(F32)).astype(BF16)
        query_all[:, cols] = query
        for h in range(start // T, (start + chunk) // T):
            at = slice(h * T - start, (h + 1) * T - start)
            weights = dot(query[:, at], keys_values[0][:, at], ((1,), (1,))) * factor[h]
            mixed[:, lanes(h)] = dot(weights.astype(BF16), keys_values[1][:, at])

    arrived(BACK_Y)
    squares = jnp.zeros((T, T), F32)
    for h in range(NY):
        at = lanes(h)
        result = mixed[:, at] + grown[h] * dot(query_all[:, at], e_in[h])
        mixed[:, at] = result
        squares = squares + result * result

    norm[hd] = jnp.broadcast_to(jnp.sum(squares.T, axis=0, keepdims=True), (8, T))
    for k in range(1, nh):
        put(norm.at[hd], norm.at[hd], NORM, h_dev(lax.rem(hd + k, nh)))
    expect(NORM, norm.at[pl.ds(0, nh - 1)], norm.at[pl.ds(0, nh - 1)])
    finish()
    square_sum = norm[0]
    for k in range(1, nh):
        square_sum = square_sum + norm[k]
    inverse = lax.rsqrt(square_sum * (1.0 / heads_total) + 1e-05)
    scale = jnp.broadcast_to(inverse[:1], (T, T)).T
    for h in range(NY):
        at = lanes(h)
        out[:, at] = (mixed[:, at] * scale * gain[:, at]).astype(BF16)


def hbm(a):
    return pltpu.with_memory_space_constraint(a, pltpu.HBM)


def local(nz, nh, text_qkv, vis_feats, w_visual, vis_src, log_decay, norm_gain):
    row_count, _, inner = text_qkv.shape
    width = vis_feats.shape[1]
    vr = vis_feats.shape[0] * NY * nz
    _, owners, _ = halves(nz)
    share = T // owners
    vmem = pl.BlockSpec(memory_space=pltpu.VMEM)
    anywhere = pl.BlockSpec(memory_space=pltpu.HBM)
    scratch = [
        pltpu.VMEM((3, row_count, inner), BF16),
        pltpu.VMEM(vis_feats.shape, BF16),
        pltpu.VMEM((3, width, inner), BF16),
        pltpu.VMEM((1, row_count), jnp.int32),
        pltpu.VMEM(log_decay.shape, F32),
        pltpu.VMEM((1, inner), F32),
        pltpu.VMEM((NY, 4 * (nh // 2), width // nh), BF16),
        pltpu.VMEM((nh, nz, 4 * NY, width // nh), BF16),
        pltpu.VMEM((2, vr, inner), F32),
        pltpu.VMEM((row_count, inner), F32),
        pltpu.VMEM((row_count, inner), BF16),
        pltpu.VMEM((NY, T, T), BF16),
        pltpu.VMEM((NY, T, T), BF16),
        pltpu.VMEM((NY, T, T), BF16),
        pltpu.VMEM((NY, T, T), BF16),
        pltpu.VMEM((NY, T, T), F32),
        pltpu.VMEM((owners, share, T), F32),
        pltpu.VMEM((nz, share, T), F32),
        pltpu.VMEM((nz, share, T), F32),
        pltpu.VMEM((owners, share, T), F32),
        pltpu.VMEM((NY, 2 * NY, T), F32),
        pltpu.VMEM((NY, NY, T), F32),
        pltpu.VMEM((nz, NY, T), F32),
        pltpu.VMEM((NY, NY, T), F32),
        pltpu.VMEM((nz, NY, vr), F32),
        pltpu.VMEM((NY, vr), F32),
        pltpu.VMEM((NY, T, vr + T), F32),
        pltpu.VMEM((NY, T, T), F32),
        pltpu.VMEM((row_count, inner), F32),
        pltpu.VMEM((nh, 8, T), F32),
        pltpu.SemaphoreType.DMA((13,)),
        pltpu.SemaphoreType.DMA((RECEIVES,)),
        pltpu.SemaphoreType.DMA((8,)),
    ]
    return pl.pallas_call(
        functools.partial(kernel, nz, nh, inner * nh),
        out_shape=jax.ShapeDtypeStruct((row_count, inner), BF16),
        in_specs=[anywhere] * 6,
        out_specs=vmem,
        scratch_shapes=scratch,
        compiler_params=pltpu.CompilerParams(
            collective_id=0, has_side_effects=True, vmem_limit_bytes=48 * 1024 * 1024
        ),
        name="lightning",
    )(
        hbm(text_qkv.transpose(1, 0, 2)),
        hbm(vis_feats),
        hbm(w_visual.transpose(1, 0, 2)),
        hbm(vis_src.reshape(1, row_count)),
        hbm(log_decay),
        hbm(norm_gain.reshape(1, inner)),
    )


def solution(mesh):
    placed = (
        P("ctx", None, "head"),
        P("ctx", None),
        P(None, None, "head"),
        P("ctx"),
        P("head", "ctx"),
        P("head"),
    )
    nz, nh = mesh.shape["ctx"] // NY, mesh.shape["head"]
    return jax.shard_map(
        functools.partial(local, nz, nh), mesh=mesh, in_specs=placed, out_specs=P("ctx", "head"), check_vma=False
    )
```
